256 devices in a mesh: tm: 8 (over z), ha: 8 (over x, core), wa: 4 (over y).
Axes of the slice: x: 4, y: 4, z: 8, core: 2. Of those that a mesh axis runs over, the one named last changes fastest.
Arguments:
- latents: bfloat16 [2, 16, 64, 32, 256], P(None, 'tm', 'ha', 'wa'), may hold values from -60 to 60, as said below
- gain_one: float32 [256], replicated, may hold values from 0.5 to 2
- shift_one: float32 [256], replicated, may hold values from -1 to 1
- kernel_one: bfloat16 [3, 3, 3, 256, 256], replicated, may hold values from -0.078125 to 0.078125
- bias_one: float32 [256], replicated, may hold values from -0.5 to 0.5
- gain_two: float32 [256], replicated, may hold values from 0.5 to 2
- shift_two: float32 [256], replicated, may hold values from -1 to 1
- kernel_two: bfloat16 [3, 3, 3, 256, 256], replicated, may hold values from -0.078125 to 0.078125
- bias_two: float32 [256], replicated, may hold values from -0.5 to 0.5
- kernel_up: bfloat16 [3, 3, 3, 256, 256], replicated, may hold values from -0.078125 to 0.078125
- bias_up: float32 [256], replicated, may hold values from -0.5 to 0.5
Outputs:
- decoded: bfloat16 [2, 16, 128, 64, 256], P(None, 'tm', 'ha', 'wa')
The draws below stay inside these ranges and needn't reach their ends.
Inputs may be any that keep to these rules, and one draw needn't show every extreme that they name: `latents`: float activations.
All inputs are finite; a program needn't handle non-finite values.
Results may differ from the reference program's by a relative error of at most 0.014.
Values may be sent and summed in bfloat16 or wider, within the bound.
A program may use at most 64 MiB of HBM per device.

```python
import math
import jax
import jax.numpy as jnp
from jax import lax

C = 256
GROUPS = 32
REQ = 2
NT = 16
NH = 64
NW = 32


def draw_latents(key, part):
    key = jax.random.fold_in(key, 11)
    key_noise, key_chan, key_rough, key_offset, key_frame, key_phase = jax.random.split(key, 6)
    shape = (REQ, NT, NH, NW, C)
    noise = jnp.clip(jax.random.normal(key_noise, shape, jnp.float32), -4.0, 4.0)
    offset = jax.random.uniform(key_offset, (C,), jnp.float32, -1.0, 1.0)
    channel_scale = jnp.exp(jax.random.uniform(key_chan, (C,), jnp.float32, math.log(0.5), math.log(2.0)))
    phases = jax.random.uniform(key_phase, (2,), jnp.float32, 0.0, 2.0 * math.pi)
    row_pos = jnp.arange(NH, dtype=jnp.float32) / NH
    col_pos = jnp.arange(NW, dtype=jnp.float32) / NW
    field = 0.5 + 0.25 * jnp.cos(2.0 * math.pi * row_pos + phases[0])[:, None] + 0.25 * jnp.cos(2.0 * math.pi * col_pos + phases[1])[None, :]
    spatial = 0.25 * jnp.exp(math.log(8.0) * field)
    rough = jnp.exp(jax.random.uniform(key_rough, (NH, NW), jnp.float32, math.log(0.7), 0.0))
    rising = jnp.exp(math.log(3.0) * jnp.arange(NT, dtype=jnp.float32) / max(NT - 1, 1))
    frame_scale = rising[None, :] * jnp.exp(jax.random.uniform(key_frame, (REQ, NT), jnp.float32, math.log(0.5), 0.0))
    place = spatial * rough
    values = (noise + offset) * channel_scale * frame_scale[:, :, None, None, None] * place[None, None, :, :, None]
    return values.astype(jnp.bfloat16)


def centred(stream_key, extent, width, bound, kind=jnp.bfloat16):
    entries = jax.random.normal(stream_key, extent, jnp.float32) * width
    return jnp.minimum(jnp.maximum(entries, -bound), bound).astype(kind)


def setup_inputs(seed: int = 0) -> dict:
    arg_keys = jax.random.split(jax.random.key(seed), 12)
    latents = draw_latents(jax.random.fold_in(arg_keys[11], 71), 0)
    gain_one = jnp.clip(jnp.exp(jax.random.uniform(arg_keys[1], (C,), jnp.float32, math.log(0.5), math.log(2.0))), 0.5, 2.0)
    shift_one = jnp.clip(jax.random.uniform(arg_keys[2], (C,), jnp.float32, -1.0, 1.0), -1.0, 1.0)
    kernel_one = centred(arg_keys[3], (3, 3, 3, C, C), (27 * C) ** -0.5, 0.078125)
    bias_one = jnp.clip(jax.random.uniform(arg_keys[4], (C,), jnp.float32, -0.5, 0.5), -0.5, 0.5)
    gain_two = jnp.clip(jnp.exp(jax.random.uniform(arg_keys[5], (C,), jnp.float32, math.log(0.5), math.log(2.0))), 0.5, 2.0)
    shift_two = jnp.clip(jax.random.uniform(arg_keys[6], (C,), jnp.float32, -1.0, 1.0), -1.0, 1.0)
    kernel_two = centred(arg_keys[7], (3, 3, 3, C, C), (27 * C) ** -0.5, 0.078125)
    bias_two = jnp.clip(jax.random.uniform(arg_keys[8], (C,), jnp.float32, -0.5, 0.5), -0.5, 0.5)
    kernel_up = centred(arg_keys[9], (3, 3, 3, C, C), (27 * C) ** -0.5, 0.078125)
    bias_up = jnp.clip(jax.random.uniform(arg_keys[10], (C,), jnp.float32, -0.5, 0.5), -0.5, 0.5)
    return {"latents": latents, "gain_one": gain_one, "shift_one": shift_one, "kernel_one": kernel_one, "bias_one": bias_one, "gain_two": gain_two, "shift_two": shift_two, "kernel_two": kernel_two, "bias_two": bias_two, "kernel_up": kernel_up, "bias_up": bias_up}


epsilon = 1e-06

def norm_silu(signal, gain, offset):
    grouped = signal.reshape(signal.shape[0], -1, GROUPS, signal.shape[-1] // GROUPS)
    centre = lax.optimization_barrier(jnp.mean(grouped, axis=(1, 3), keepdims=True))
    variance = lax.optimization_barrier(jnp.mean(jnp.square(grouped - centre), axis=(1, 3), keepdims=True))
    normed = ((grouped - centre) * lax.rsqrt(variance + epsilon)).reshape(signal.shape)
    return jax.nn.silu(normed * gain + offset).astype(jnp.bfloat16)

def causal_conv(signal, kernel, bias):
    batch, frames, rows_in, cols_in, channels = signal.shape
    padded = jnp.pad(signal, ((0, 0), (2, 0), (1, 1), (1, 1), (0, 0)))
    result = jnp.zeros((batch * frames * rows_in * cols_in, kernel.shape[-1]), jnp.float32)
    for tap_t in range(3):
        for tap_h in range(3):
            for tap_w in range(3):
                window = padded[:, tap_t:tap_t + frames, tap_h:tap_h + rows_in, tap_w:tap_w + cols_in].reshape(-1, channels)
                result = result + jnp.dot(window, kernel[tap_t, tap_h, tap_w], preferred_element_type=jnp.float32)
    return result.reshape(batch, frames, rows_in, cols_in, -1) + bias

def reference(latents, gain_one, shift_one, kernel_one, bias_one, gain_two, shift_two, kernel_two, bias_two, kernel_up, bias_up):
    act_one = norm_silu(latents.astype(jnp.float32), gain_one, shift_one)
    hidden = causal_conv(act_one, kernel_one, bias_one).astype(jnp.bfloat16)
    hidden = lax.optimization_barrier(hidden)
    act_two = norm_silu(hidden.astype(jnp.float32), gain_two, shift_two)
    residual = (causal_conv(act_two, kernel_two, bias_two) + latents.astype(jnp.float32)).astype(jnp.bfloat16)
    enlarged = jnp.repeat(jnp.repeat(residual, 2, axis=2), 2, axis=3)
    return causal_conv(enlarged, kernel_up, bias_up).astype(jnp.bfloat16)
```

```python
import functools

import jax
import jax.numpy as jnp
from jax import lax
from jax.experimental import pallas as pl
from jax.experimental.pallas import tpu as pltpu
from jax.sharding import PartitionSpec as P

MESH = pl.DeviceIdType.MESH
AXES = ("tm", "ha", "wa")
GROUP = 8
EPS = 1e-6
F32, BF16 = jnp.float32, jnp.bfloat16
CH = 256


def lanes(shape):
    return lax.broadcasted_iota(jnp.int32, shape, len(shape) - 1)


def group_sum(x):
    lane = lanes(x.shape)
    for s in (1, 2, 4):
        x = x + jnp.where((lane // s) % 2 == 0, pltpu.roll(x, 128 - s, 1), pltpu.roll(x, s, 1))
    return x


def halves(x):
    return jnp.concatenate([x[:, :128], x[:, 128:]], axis=0)


def whole(x, clip):
    return jnp.concatenate([x[clip : clip + 1], x[2 + clip : 3 + clip]], axis=1)


def moments(tile, count):
    sums = jnp.sum(jnp.sum(tile, axis=(0, 1)), axis=1)
    mean = group_sum(halves(sums)) * (1.0 / count)
    centre = jnp.stack([whole(mean, 0), whole(mean, 1)])
    dev = tile - centre[None, None]
    spread = group_sum(halves(jnp.sum(jnp.sum(dev * dev, axis=(0, 1)), axis=1)))
    rows = jnp.concatenate([mean[0:2], spread[0:2], mean[2:4], spread[2:4]], axis=0)
    pick = lanes((8, 128)) % 8 == lax.broadcasted_iota(jnp.int32, (8, 128), 0)
    return jnp.sum(jnp.where(pick, rows, 0.0), axis=0, keepdims=True)


def merge(rows, count):
    n = rows.shape[0]
    total = jnp.sum(rows, axis=0)
    mean = total * (1.0 / n)
    dev = rows - mean[None]
    apart = jnp.sum(dev * dev, axis=0)
    return jnp.where(lanes((1, 128)) % 4 < 2, mean, total + float(count) * pltpu.roll(apart, 2, 1))


def spread_out(row, total):
    pick = lanes((8, 128)) % 8 == lax.broadcasted_iota(jnp.int32, (8, 128), 0)
    v = group_sum(jnp.where(pick, row, 0.0))
    mean = [jnp.concatenate([v[c : c + 1], v[4 + c : 5 + c]], axis=1) for c in (0, 1)]
    m2 = [jnp.concatenate([v[2 + c : 3 + c], v[6 + c : 7 + c]], axis=1) for c in (0, 1)]
    return mean, [lax.rsqrt(m * (1.0 / total) + EPS) for m in m2]


def silu(u):
    return u * (0.5 + 0.5 * jnp.tanh(0.5 * u))


def body(sizes, lat, gain1, shift1, k1, bias1, gain2, shift2, k2, bias2, ku, bias_up, out,
         xv, cb, sl, sx, xr, cp, ss, sf, ab, k1v, k2v, kuv, kuc, fbuf, acc, ob, g1, g2,
         lsem, ssem, rsem, gsend, grecv):
    nt, nh, nw = sizes
    it, ih, iw = (lax.axis_index(a) for a in AXES)

    def at(dt, dh, dw):
        return (lax.rem(it + dt % nt, nt), lax.rem(ih + dh % nh, nh), lax.rem(iw + dw % nw, nw))

    def ring(d, n):
        return min(d, n - d)

    plane = sorted(
        [(0, a, b) for a in range(nh) for b in range(nw) if a or b],
        key=lambda o: -(ring(o[1], nh) + 2 * ring(o[2], nw)),
    )
    line = sorted([(a, 0, 0) for a in range(1, nt)], key=lambda o: -ring(o[0], nt))

    loads = [
        pltpu.make_async_copy(s, d, lsem.at[i])
        for i, (s, d) in enumerate(((lat, xv), (k1, k1v), (ku, kuv), (k2, k2v)))
    ]
    loads[0].start()
    barrier = pltpu.get_barrier_semaphore()
    for o in plane + line:
        pl.semaphore_signal(barrier, inc=1, device_id=at(*o), device_id_type=MESH)
    for c in loads[1:]:
        c.start()

    sends = []

    def send(e, slot, src, dst, offset):
        c = pltpu.make_async_remote_copy(
            src_ref=src, dst_ref=dst, send_sem=ssem.at[e, slot], recv_sem=rsem.at[e, slot],
            device_id=at(*offset), device_id_type=MESH)
        c.start()
        sends.append(c)
        return c

    def edges(e):
        for half in (0, 1):
            cols = pl.ds(half * 128, 128)
            left = fbuf[half, pl.ds(0, 32, stride=8), :]
            right = fbuf[half, pl.ds(7, 32, stride=8), :]
            ss[e, 0, :, cols] = left.astype(BF16)
            ss[e, 1, :, cols] = right.astype(BF16)
            parts = []
            for h in (0, 14):
                for side in (left, right):
                    parts += [side[h : h + 2], side[16 + h : 18 + h]]
            sx[e, :, cols] = jnp.concatenate(parts, axis=0).astype(BF16)

    def near(e):
        own = pl.ds(2, 2)
        return [
            send(e, 0, cb.at[e, own, 1], cb.at[e, own, 9], (0, -1, 0)),
            send(e, 1, cb.at[e, own, 8], cb.at[e, own, 0], (0, 1, 0)),
            send(e, 2, ss.at[e, 0], sl.at[e, 1, 1], (0, 0, -1)),
            send(e, 3, ss.at[e, 1], sl.at[e, 1, 0], (0, 0, 1)),
            send(e, 4, sx.at[e], xr.at[e, 0], (0, -1, -1)),
            send(e, 5, sx.at[e], xr.at[e, 1], (0, -1, 1)),
            send(e, 6, sx.at[e], xr.at[e, 2], (0, 1, -1)),
            send(e, 7, sx.at[e], xr.at[e, 3], (0, 1, 1)),
        ]

    def tile_on(e):
        return send(e, 8, cb.at[e, pl.ds(2, 2), pl.ds(1, 8)], cb.at[e, pl.ds(0, 2), pl.ds(1, 8)], (1, 0, 0))

    def rims_on(e, arrivals):
        for c in arrivals:
            c.wait_recv()
        block = lax.broadcasted_iota(jnp.int32, (16, CH), 0) // 4
        tiles = [xr[e, d].astype(F32) for d in range(4)]
        picked = jnp.where(
            block == 0, tiles[0], jnp.where(block == 1, tiles[1], jnp.where(block == 2, tiles[2], tiles[3]))
        )
        cp[e, 1] = picked.astype(BF16)
        prev, own = pl.ds(0, 2), pl.ds(2, 2)
        return [
            send(e, 9, cb.at[e, own, 0], cb.at[e, prev, 0], (1, 0, 0)),
            send(e, 10, cb.at[e, own, 9], cb.at[e, prev, 9], (1, 0, 0)),
            send(e, 11, sl.at[e, 1], sl.at[e, 0], (1, 0, 0)),
            send(e, 12, cp.at[e, 1], cp.at[e, 0], (1, 0, 0)),
        ]

    def gather(e, phase, buf, row, offsets):
        buf[e, 0] = row
        for slot, o in enumerate(offsets):
            pltpu.make_async_remote_copy(
                src_ref=buf.at[e, 0], dst_ref=buf.at[e, 1 + slot], send_sem=gsend.at[e, phase],
                recv_sem=grecv.at[e, phase], device_id=at(*o), device_id_type=MESH).start()

    def gathered(e, phase, buf, offsets):
        peers = buf.at[e, pl.ds(1, len(offsets))]
        c = pltpu.make_async_remote_copy(
            src_ref=peers, dst_ref=peers, send_sem=gsend.at[e, phase], recv_sem=grecv.at[e, phase],
            device_id=at(1, 0, 0), device_id_type=MESH)
        c.wait_recv()
        sends.append(c)
        return buf[e]

    def fill(e, frames, norm):
        lo, hi = frames
        pairs = [p for p in (0, 1) if lo <= 2 * p < hi]
        if norm is not None:
            mean, scale, shift = norm
            parity = lax.broadcasted_iota(jnp.int32, (8, CH), 0) % 2 == 0
            mean8 = jnp.where(parity, mean[0], mean[1])
            scale8 = jnp.where(parity, scale[0], scale[1])
            mean2, scale2 = jnp.stack(mean), jnp.stack(scale)

        def act8(x):
            return x if norm is None else silu((x - mean8) * scale8 + shift)

        for p in pairs:
            here = (it > 0) if p == 0 else (it >= 0)
            for side in (0, 1):
                there = jnp.logical_and(here, (iw > 0) if side == 0 else (iw < nw - 1))
                v = act8(sl[e, p, side].astype(F32).reshape(4, 8, CH))
                v = jnp.where(there, v, 0.0).reshape(2, 16, CH)
                for t in (0, 1):
                    sf[side, 2 * p + t, pl.ds(2, 16), :] = v[t]
            v = act8(cp[e, p].astype(F32).reshape(2, 8, CH)).reshape(16, CH)
            for k in range(4):
                above, side = k >= 2, 0 if k % 2 == 1 else 1
                there = jnp.logical_and(here, (ih > 0) if above else (ih < nh - 1))
                there = jnp.logical_and(there, (iw > 0) if side == 0 else (iw < nw - 1))
                w = jnp.where(there, v[4 * k : 4 * k + 4], 0.0)
                for t in (0, 1):
                    sf[side, 2 * p + t, pl.ds(0 if above else 18, 2), :] = w[2 * t : 2 * t + 2]

        sub = lax.broadcasted_iota(jnp.int32, (2, 8, CH), 1)

        def step(n, _):
            t, h = n // 10, n % 10
            there = jnp.logical_or(t >= 2, it > 0)
            there = jnp.logical_and(there, jnp.logical_or(h > 0, ih > 0))
            there = jnp.logical_and(there, jnp.logical_or(h < 9, ih < nh - 1))
            x = cb[e, t, h].astype(F32).reshape(2, 8, CH)
            if norm is not None:
                x = silu((x - mean2) * scale2 + shift[None])
            x = jnp.where(there, x, 0.0)
            rims = [
                jnp.stack([sf[side, t, pl.ds(2 * h + c, 1), :] for c in (0, 1)])
                for side in (0, 1)
            ]
            before = jnp.where(sub == 0, rims[0], pltpu.roll(x, 1, 1))
            after = jnp.where(sub == 7, rims[1], pltpu.roll(x, 7, 1))
            for k, v in enumerate((before, x, after)):
                ab[t, h, :, pl.ds(k * CH, CH)] = v.reshape(16, CH).astype(BF16)
            return 0

        lax.fori_loop(10 * lo, 10 * hi, step, 0)

    def conv(kv):
        total = None
        for i in range(3):
            for j in range(3):
                part = jnp.dot(
                    ab[i : i + 2, j : j + 8].reshape(256, 3 * CH), kv[3 * i + j], preferred_element_type=F32
                )
                total = part if total is None else total + part
        return total

    def keep(e, value):
        cb[e, 2:4, 1:9] = value.reshape(2, 8, 16, CH).astype(BF16)
        fbuf[0] = value[:, :128]
        fbuf[1] = value[:, 128:]

    def fold():
        def step(n, _):
            t, rows = n // 16, pl.ds(pl.multiple_of((n % 16) * 16, 16), 16)
            cols = []
            for i in range(3):
                k = [kuv[t * 3 + i, j, rows, :].astype(F32) for j in range(3)]
                cols.append((k[0], k[1] + k[2], k[0] + k[1], k[2]))
            for c in range(4):
                v = [cols[i][c] for i in range(3)]
                for r, w in enumerate((v[0], v[1] + v[2], v[0] + v[1], v[2])):
                    kuc[(r // 2) * 2 + c // 2, t, r % 2, c % 2, rows, :] = w.astype(BF16)
            return 0

        lax.fori_loop(0, 48, step, 0)

    cells = 2 * 8 * 8
    total = cells * GROUP * nt * nh * nw
    loads[0].wait()
    x = jnp.stack([xv[c].astype(F32).reshape(2, 8, 8, CH) for c in (0, 1)], axis=2)
    keep(0, x.reshape(256, CH))
    row = moments(x, cells * GROUP)
    edges(0)
    pl.semaphore_wait(barrier, len(plane) + len(line))
    gather(0, 0, g1, row, plane)
    arrivals = near(0)
    onward = [tile_on(0)]
    row = merge(gathered(0, 0, g1, plane), cells * GROUP)
    gather(0, 1, g2, row, line)
    onward += rims_on(0, arrivals)
    loads[2].wait()
    fold()
    row = merge(gathered(0, 1, g2, line), cells * GROUP * nh * nw)
    mean, rstd = spread_out(row, total)
    for c in onward:
        c.wait_recv()
    fill(0, (0, 4), (mean, [r * gain1[...] for r in rstd], shift1[...]))
    loads[1].wait()
    hidden = (conv(k1v) + bias1[...]).astype(BF16).astype(F32)

    keep(1, hidden)
    row = moments(hidden.reshape(2, 8, 2, 8, CH), cells * GROUP)
    gather(1, 0, g1, row, plane)
    edges(1)
    arrivals = near(1)
    onward = [tile_on(1)]
    row = merge(gathered(1, 0, g1, plane), cells * GROUP)
    gather(1, 1, g2, row, line)
    onward += rims_on(1, arrivals)
    row = merge(gathered(1, 1, g2, line), cells * GROUP * nh * nw)
    mean, rstd = spread_out(row, total)
    for c in onward:
        c.wait_recv()
    fill(1, (0, 4), (mean, [r * gain2[...] for r in rstd], shift2[...]))
    loads[3].wait()
    skip = cb[0, 2:4, 1:9].astype(F32).reshape(256, CH)
    residual = (conv(k2v) + bias2[...] + skip).astype(BF16).astype(F32)

    keep(2, residual)
    onward = [tile_on(2)]
    edges(2)
    arrivals = near(2)
    onward += rims_on(2, arrivals)
    fill(2, (2, 4), None)
    up = bias_up[...]

    def window(t0, t1, a, b, r):
        return ab[t0:t1, a + r : a + r + 8, :, b * CH : (b + 2) * CH].reshape(128 * (t1 - t0), 2 * CH)

    def weight(a, b, i, r):
        return kuc[2 * a + b, i, r].reshape(2 * CH, CH)

    for a in (0, 1):
        for b in (0, 1):
            both = sum(jnp.dot(window(2, 4, a, b, r), weight(a, b, 2, r), preferred_element_type=F32) for r in (0, 1))
            late = sum(jnp.dot(window(2, 3, a, b, r), weight(a, b, 1, r), preferred_element_type=F32) for r in (0, 1))
            acc[2 * a + b, 0:128] = both[0:128] + up
            acc[2 * a + b, 128:256] = both[128:256] + late + up
    for c in onward:
        c.wait_recv()
    fill(2, (0, 2), None)
    for a in (0, 1):
        for b in (0, 1):
            both = sum(jnp.dot(window(0, 2, a, b, r), weight(a, b, 0, r), preferred_element_type=F32) for r in (0, 1))
            early = sum(jnp.dot(window(1, 2, a, b, r), weight(a, b, 1, r), preferred_element_type=F32) for r in (0, 1))
            done = [both[0:128] + early + acc[2 * a + b, 0:128], both[128:256] + acc[2 * a + b, 128:256]]
            for t in (0, 1):
                for half in (0, 1):
                    ob[a, half, pl.ds(256 * t + b, 128, stride=2), :] = done[t][:, half * 128 : half * 128 + 128]
        def put(n, _):
            t, h, c = n // 16, (n // 2) % 8, n % 2
            rows = pl.ds(pl.multiple_of(n * 16, 16), 16)
            for half in (0, 1):
                out[c, t, 2 * h + a, :, pl.ds(half * 128, 128)] = ob[a, half, rows, :].astype(BF16)
            return 0

        lax.fori_loop(0, 32, put, 0)
    for c in sends:
        c.wait_send()


def shards(sizes, latents, gain1, shift1, k1, bias1, gain2, shift2, k2, bias2, ku, bias_up):
    nt, nh, nw = sizes
    row = lambda v: v.reshape(1, CH)
    vmem = pl.BlockSpec(memory_space=pltpu.VMEM)
    hbm = pl.BlockSpec(memory_space=pl.ANY)
    s = pltpu.VMEM
    return pl.pallas_call(
        functools.partial(body, sizes),
        out_shape=jax.ShapeDtypeStruct((2, 2, 16, 16, CH), BF16),
        in_specs=[hbm, vmem, vmem, hbm, vmem, vmem, vmem, hbm, vmem, hbm, vmem],
        out_specs=vmem,
        scratch_shapes=[
            s((2, 2, 64, CH), BF16),
            s((3, 4, 10, 16, CH), BF16),
            s((3, 2, 2, 32, CH), BF16),
            s((3, 16, CH), BF16),
            s((3, 4, 16, CH), BF16),
            s((3, 2, 16, CH), BF16),
            s((3, 2, 32, CH), BF16),
            s((2, 4, 20, CH), F32),
            s((4, 10, 16, 3 * CH), BF16),
            s((9, 3 * CH, CH), BF16),
            s((9, 3 * CH, CH), BF16),
            s((9, 3, CH, CH), BF16),
            s((4, 3, 2, 2, CH, CH), BF16),
            s((2, 256, 128), F32),
            s((4, 256, CH), F32),
            s((2, 2, 512, 128), F32),
            s((2, nh * nw, 1, 128), F32),
            s((2, nt, 1, 128), F32),
            pltpu.SemaphoreType.DMA((4,)),
            pltpu.SemaphoreType.DMA((3, 13)),
            pltpu.SemaphoreType.DMA((3, 13)),
            pltpu.SemaphoreType.DMA((2, 2)),
            pltpu.SemaphoreType.DMA((2, 2)),
        ],
        compiler_params=pltpu.CompilerParams(
            collective_id=0, has_side_effects=True, vmem_limit_bytes=56 * 2**20
        ),
        name="upblock",
    )(
        latents.reshape(2, 2, 64, CH), row(gain1), row(shift1), k1.reshape(9, 3 * CH, CH), row(bias1),
        row(gain2), row(shift2), k2.reshape(9, 3 * CH, CH), row(bias2), ku.reshape(9, 3, CH, CH), row(bias_up),
    )


def solution(mesh):
    sizes = tuple(mesh.shape[a] for a in AXES)
    in_specs = (P(None, "tm", "ha", "wa", None),) + (P(),) * 10
    return jax.shard_map(
        functools.partial(shards, sizes),
        mesh=mesh,
        in_specs=in_specs,
        out_specs=P(None, "tm", "ha", "wa", None),
        check_vma=False,
    )
```

```python
import functools

import jax
import jax.numpy as jnp
from jax import lax
from jax.experimental import pallas as pl
from jax.experimental.pallas import tpu as pltpu
from jax.sharding import PartitionSpec as P

MESH = pl.DeviceIdType.MESH
AXES = ("tm", "ha", "wa")
GROUP = 8
EPS = 1e-6
F32, BF16 = jnp.float32, jnp.bfloat16
CH = 256


def lanes(shape):
    return lax.broadcasted_iota(jnp.int32, shape, len(shape) - 1)


def group_sum(x):
    lane = lanes(x.shape)
    for s in (1, 2, 4):
        x = x + jnp.where((lane // s) % 2 == 0, pltpu.roll(x, 128 - s, 1), pltpu.roll(x, s, 1))
    return x


def halves(x):
    return jnp.concatenate([x[:, :128], x[:, 128:]], axis=0)


def whole(x, clip):
    return jnp.concatenate([x[clip : clip + 1], x[2 + clip : 3 + clip]], axis=1)


def moments(tile, count):
    sums = jnp.sum(jnp.sum(tile, axis=(0, 1)), axis=1)
    mean = group_sum(halves(sums)) * (1.0 / count)
    centre = jnp.stack([whole(mean, 0), whole(mean, 1)])
    dev = tile - centre[None, None]
    spread = group_sum(halves(jnp.sum(jnp.sum(dev * dev, axis=(0, 1)), axis=1)))
    rows = jnp.concatenate([mean[0:2], spread[0:2], mean[2:4], spread[2:4]], axis=0)
    pick = lanes((8, 128)) % 8 == lax.broadcasted_iota(jnp.int32, (8, 128), 0)
    return jnp.sum(jnp.where(pick, rows, 0.0), axis=0, keepdims=True)


def merge(rows, count):
    n = rows.shape[0]
    total = jnp.sum(rows, axis=0)
    mean = total * (1.0 / n)
    dev = rows - mean[None]
    apart = jnp.sum(dev * dev, axis=0)
    return jnp.where(lanes((1, 128)) % 4 < 2, mean, total + float(count) * pltpu.roll(apart, 2, 1))


def spread_out(row, total):
    pick = lanes((8, 128)) % 8 == lax.broadcasted_iota(jnp.int32, (8, 128), 0)
    v = group_sum(jnp.where(pick, row, 0.0))
    mean = [jnp.concatenate([v[c : c + 1], v[4 + c : 5 + c]], axis=1) for c in (0, 1)]
    m2 = [jnp.concatenate([v[2 + c : 3 + c], v[6 + c : 7 + c]], axis=1) for c in (0, 1)]
    return mean, [lax.rsqrt(m * (1.0 / total) + EPS) for m in m2]


def silu(u):
    return u * (0.5 + 0.5 * jnp.tanh(0.5 * u))


def body(sizes, lat, gain1, shift1, k1, bias1, gain2, shift2, k2, bias2, ku, bias_up, out,
         xv, cb, sl, sx, xr, cp, ss, sf, ab, k1v, k2v, kuv, kuc, fbuf, acc, ob, g1, g2, g3, g4,
         lsem, ssem, rsem, gsend, grecv):
    nt, nh, nw = sizes
    it, ih, iw = (lax.axis_index(a) for a in AXES)

    def at(dt, dh, dw):
        if dh is None:
            return (it, ih + 1 - 2 * lax.rem(ih, 2), iw)
        return (lax.rem(it + dt % nt, nt), lax.rem(ih + dh % nh, nh), lax.rem(iw + dw % nw, nw))

    def ring(d, n):
        return min(d, n - d)

    plane = sorted(
        [(0, a, b) for a in range(nh) for b in range(nw) if a or b],
        key=lambda o: -(ring(o[1], nh) + 2 * ring(o[2], nw)),
    )
    line = sorted([(a, 0, 0) for a in range(1, nt)], key=lambda o: -ring(o[0], nt))

    pair = [(0, None, 0)]
    chips = sorted(
        [(a, 2 * b, c) for a in range(nt) for b in range(nh // 2) for c in range(nw) if a or b or c],
        key=lambda o: -(ring(o[0], nt) + ring(o[1], nh) // 2 + ring(o[2], nw)),
    )

    loads = [
        pltpu.make_async_copy(s, d, lsem.at[i])
        for i, (s, d) in enumerate(((lat, xv), (k1, k1v), (ku, kuv), (k2, k2v)))
    ]
    loads[0].start()
    barrier = pltpu.get_barrier_semaphore()
    for o in plane + line:
        pl.semaphore_signal(barrier, inc=1, device_id=at(*o), device_id_type=MESH)
    for c in loads[1:]:
        c.start()

    sends = []

    def send(e, slot, src, dst, offset):
        c = pltpu.make_async_remote_copy(
            src_ref=src, dst_ref=dst, send_sem=ssem.at[e, slot], recv_sem=rsem.at[e, slot],
            device_id=at(*offset), device_id_type=MESH)
        c.start()
        sends.append(c)
        return c

    def edges(e):
        for half in (0, 1):
            cols = pl.ds(half * 128, 128)
            left = fbuf[half, pl.ds(0, 32, stride=8), :]
            right = fbuf[half, pl.ds(7, 32, stride=8), :]
            ss[e, 0, :, cols] = left.astype(BF16)
            ss[e, 1, :, cols] = right.astype(BF16)
            parts = []
            for h in (0, 14):
                for side in (left, right):
                    parts += [side[h : h + 2], side[16 + h : 18 + h]]
            sx[e, :, cols] = jnp.concatenate(parts, axis=0).astype(BF16)

    def near(e):
        own = pl.ds(2, 2)
        return [
            send(e, 0, cb.at[e, own, 1], cb.at[e, own, 9], (0, -1, 0)),
            send(e, 1, cb.at[e, own, 8], cb.at[e, own, 0], (0, 1, 0)),
            send(e, 2, ss.at[e, 0], sl.at[e, 1, 1], (0, 0, -1)),
            send(e, 3, ss.at[e, 1], sl.at[e, 1, 0], (0, 0, 1)),
            send(e, 4, sx.at[e], xr.at[e, 0], (0, -1, -1)),
            send(e, 5, sx.at[e], xr.at[e, 1], (0, -1, 1)),
            send(e, 6, sx.at[e], xr.at[e, 2], (0, 1, -1)),
            send(e, 7, sx.at[e], xr.at[e, 3], (0, 1, 1)),
        ]

    def tile_on(e):
        return send(e, 8, cb.at[e, pl.ds(2, 2), pl.ds(1, 8)], cb.at[e, pl.ds(0, 2), pl.ds(1, 8)], (1, 0, 0))

    def frame_on(e, t):
        rows = pl.ds(1, 8)
        return send(e, 8 if t == 0 else 13, cb.at[e, 2 + t, rows], cb.at[e, t, rows], (1, 0, 0))

    def rims_on(e, arrivals):
        for c in arrivals:
            c.wait_recv()
        block = lax.broadcasted_iota(jnp.int32, (16, CH), 0) // 4
        tiles = [xr[e, d].astype(F32) for d in range(4)]
        picked = jnp.where(
            block == 0, tiles[0], jnp.where(block == 1, tiles[1], jnp.where(block == 2, tiles[2], tiles[3]))
        )
        cp[e, 1] = picked.astype(BF16)
        prev, own = pl.ds(0, 2), pl.ds(2, 2)
        return [
            send(e, 9, cb.at[e, own, 0], cb.at[e, prev, 0], (1, 0, 0)),
            send(e, 10, cb.at[e, own, 9], cb.at[e, prev, 9], (1, 0, 0)),
            send(e, 11, sl.at[e, 1], sl.at[e, 0], (1, 0, 0)),
            send(e, 12, cp.at[e, 1], cp.at[e, 0], (1, 0, 0)),
        ]

    def gather(e, phase, buf, row, offsets):
        buf[0] = row
        for slot, o in enumerate(offsets):
            pltpu.make_async_remote_copy(
                src_ref=buf.at[0], dst_ref=buf.at[1 + slot], send_sem=gsend.at[e, phase],
                recv_sem=grecv.at[e, phase], device_id=at(*o), device_id_type=MESH).start()

    def gathered(e, phase, buf, offsets):
        peers = buf.at[pl.ds(1, len(offsets))]
        c = pltpu.make_async_remote_copy(
            src_ref=peers, dst_ref=peers, send_sem=gsend.at[e, phase], recv_sem=grecv.at[e, phase],
            device_id=at(1, 0, 0), device_id_type=MESH)
        c.wait_recv()
        sends.append(c)
        return buf[...]

    def fill(e, frames, norm):
        lo, hi = frames
        pairs = [p for p in (0, 1) if lo <= 2 * p < hi]
        if norm is not None:
            mean, scale, shift = norm
            parity = lax.broadcasted_iota(jnp.int32, (8, CH), 0) % 2 == 0
            mean8 = jnp.where(parity, mean[0], mean[1])
            scale8 = jnp.where(parity, scale[0], scale[1])
            mean2, scale2 = jnp.stack(mean), jnp.stack(scale)

        def act8(x):
            return x if norm is None else silu((x - mean8) * scale8 + shift)

        for p in pairs:
            here = (it > 0) if p == 0 else (it >= 0)
            for side in (0, 1):
                there = jnp.logical_and(here, (iw > 0) if side == 0 else (iw < nw - 1))
                v = act8(sl[e, p, side].astype(F32).reshape(4, 8, CH))
                v = jnp.where(there, v, 0.0).reshape(2, 16, CH)
                for t in (0, 1):
                    sf[side, 2 * p + t, pl.ds(2, 16), :] = v[t]
            v = act8(cp[e, p].astype(F32).reshape(2, 8, CH)).reshape(16, CH)
            for k in range(4):
                above, side = k >= 2, 0 if k % 2 == 1 else 1
                there = jnp.logical_and(here, (ih > 0) if above else (ih < nh - 1))
                there = jnp.logical_and(there, (iw > 0) if side == 0 else (iw < nw - 1))
                w = jnp.where(there, v[4 * k : 4 * k + 4], 0.0)
                for t in (0, 1):
                    sf[side, 2 * p + t, pl.ds(0 if above else 18, 2), :] = w[2 * t : 2 * t + 2]

        sub = lax.broadcasted_iota(jnp.int32, (2, 8, CH), 1)

        for n in range(10 * lo, 10 * hi):
            t, h = n // 10, n % 10
            there = None if t >= 2 else it > 0
            if h in (0, 9):
                row = (ih > 0) if h == 0 else (ih < nh - 1)
                there = row if there is None else jnp.logical_and(there, row)
            x = cb[e, t, h].astype(F32).reshape(2, 8, CH)
            if norm is not None:
                x = silu((x - mean2) * scale2 + shift[None])
            if there is not None:
                x = jnp.where(there, x, 0.0)
            rims = [
                jnp.stack([sf[side, t, pl.ds(2 * h + c, 1), :] for c in (0, 1)])
                for side in (0, 1)
            ]
            before = jnp.where(sub == 0, rims[0], pltpu.roll(x, 1, 1))
            after = jnp.where(sub == 7, rims[1], pltpu.roll(x, 7, 1))
            for k, v in enumerate((before, x, after)):
                ab[t, h, :, pl.ds(k * CH, CH)] = v.reshape(16, CH).astype(BF16)

    def conv(kv, t0, t1):
        total = None
        for i in range(3):
            for j in range(3):
                part = jnp.dot(
                    ab[i + t0 : i + t1, j : j + 8].reshape(128 * (t1 - t0), 3 * CH), kv[3 * i + j], preferred_element_type=F32
                )
                total = part if total is None else total + part
        return total

    def keep(e, value, t0, t1):
        cb[e, 2 + t0 : 2 + t1, 1:9] = value.reshape(t1 - t0, 8, 16, CH).astype(BF16)
        fbuf[0, 128 * t0 : 128 * t1] = value[:, :128]
        fbuf[1, 128 * t0 : 128 * t1] = value[:, 128:]

    def fold():
        def step(n, _):
            t, rows = n // 16, pl.ds(pl.multiple_of((n % 16) * 16, 16), 16)
            cols = []
            for i in range(3):
                k = [kuv[t * 3 + i, j, rows, :].astype(F32) for j in range(3)]
                cols.append((k[0], k[1] + k[2], k[0] + k[1], k[2]))
            for c in range(4):
                v = [cols[i][c] for i in range(3)]
                for r, w in enumerate((v[0], v[1] + v[2], v[0] + v[1], v[2])):
                    kuc[(r // 2) * 2 + c // 2, t, r % 2, c % 2, rows, :] = w.astype(BF16)
            return 0

        lax.fori_loop(0, 48, step, 0)

    cells = 2 * 8 * 8
    total = cells * GROUP * nt * nh * nw
    loads[0].wait()
    x = jnp.stack([xv[c].astype(F32).reshape(2, 8, 8, CH) for c in (0, 1)], axis=2)
    row = moments(x, cells * GROUP)
    keep(0, x.reshape(256, CH), 0, 2)
    pl.semaphore_wait(barrier, len(plane) + len(line))
    gather(0, 0, g1, row, plane)
    edges(0)
    arrivals = near(0)
    onward = [tile_on(0)]
    row = merge(gathered(0, 0, g1, plane), cells * GROUP)
    gather(0, 1, g2, row, line)
    onward += rims_on(0, arrivals)
    loads[2].wait()
    fold()
    row = merge(gathered(0, 1, g2, line), cells * GROUP * nh * nw)
    mean, rstd = spread_out(row, total)
    for c in onward:
        c.wait_recv()
    fill(0, (0, 4), (mean, [r * gain1[...] for r in rstd], shift1[...]))
    loads[1].wait()
    hidden = (conv(k1v, 0, 2) + bias1[...]).astype(BF16).astype(F32)

    row = moments(hidden.reshape(2, 8, 2, 8, CH), cells * GROUP)
    gather(1, 0, g3, row, pair)
    keep(1, hidden, 0, 2)
    edges(1)
    row = merge(gathered(1, 0, g3, pair), cells * GROUP)
    gather(1, 1, g4, row, chips)
    arrivals = near(1)
    onward = [tile_on(1)]
    onward += rims_on(1, arrivals)
    row = merge(gathered(1, 1, g4, chips), cells * GROUP * 2)
    mean, rstd = spread_out(row, total)
    for c in onward:
        c.wait_recv()
    fill(1, (0, 4), (mean, [r * gain2[...] for r in rstd], shift2[...]))
    loads[3].wait()
    onward = []
    for t in (0, 1):
        skip = cb[0, 2 + t, 1:9].astype(F32).reshape(128, CH)
        residual = (conv(k2v, t, t + 1) + bias2[...] + skip).astype(BF16).astype(F32)
        keep(2, residual, t, t + 1)
        onward.append(frame_on(2, t))
    edges(2)
    arrivals = near(2)
    onward += rims_on(2, arrivals)
    fill(2, (2, 4), None)
    up = bias_up[...]

    def window(t0, t1, a, b, r):
        return ab[t0:t1, a + r : a + r + 8, :, b * CH : (b + 2) * CH].reshape(128 * (t1 - t0), 2 * CH)

    def weight(a, b, i, r):
        return kuc[2 * a + b, i, r].reshape(2 * CH, CH)

    for a in (0, 1):
        for b in (0, 1):
            both = sum(jnp.dot(window(2, 4, a, b, r), weight(a, b, 2, r), preferred_element_type=F32) for r in (0, 1))
            late = sum(jnp.dot(window(2, 3, a, b, r), weight(a, b, 1, r), preferred_element_type=F32) for r in (0, 1))
            acc[2 * a + b, 0:128] = both[0:128] + up
            acc[2 * a + b, 128:256] = both[128:256] + late + up
    for c in onward:
        c.wait_recv()
    fill(2, (0, 2), None)
    for a in (0, 1):
        for b in (0, 1):
            both = sum(jnp.dot(window(0, 2, a, b, r), weight(a, b, 0, r), preferred_element_type=F32) for r in (0, 1))
            early = sum(jnp.dot(window(1, 2, a, b, r), weight(a, b, 1, r), preferred_element_type=F32) for r in (0, 1))
            done = [both[0:128] + early + acc[2 * a + b, 0:128], both[128:256] + acc[2 * a + b, 128:256]]
            for t in (0, 1):
                for half in (0, 1):
                    ob[a, half, pl.ds(256 * t + b, 128, stride=2), :] = done[t][:, half * 128 : half * 128 + 128]
        for n in range(32):
            t, h, c = n // 16, (n // 2) % 8, n % 2
            for half in (0, 1):
                out[c, t, 2 * h + a, :, pl.ds(half * 128, 128)] = ob[a, half, pl.ds(16 * n, 16), :].astype(BF16)
    for c in sends:
        c.wait_send()


def shards(sizes, latents, gain1, shift1, k1, bias1, gain2, shift2, k2, bias2, ku, bias_up):
    nt, nh, nw = sizes
    row = lambda v: v.reshape(1, CH)
    vmem = pl.BlockSpec(memory_space=pltpu.VMEM)
    hbm = pl.BlockSpec(memory_space=pl.ANY)
    s = pltpu.VMEM
    return pl.pallas_call(
        functools.partial(body, sizes),
        out_shape=pltpu.VMEM((2, 2, 16, 16, CH), BF16),
        in_specs=[hbm, vmem, vmem, hbm, vmem, vmem, vmem, hbm, vmem, hbm, vmem],
        out_specs=vmem,
        scratch_shapes=[
            s((2, 2, 64, CH), BF16),
            s((3, 4, 10, 16, CH), BF16),
            s((3, 2, 2, 32, CH), BF16),
            s((3, 16, CH), BF16),
            s((3, 4, 16, CH), BF16),
            s((3, 2, 16, CH), BF16),
            s((3, 2, 32, CH), BF16),
            s((2, 4, 20, CH), F32),
            s((4, 10, 16, 3 * CH), BF16),
            s((9, 3 * CH, CH), BF16),
            s((9, 3 * CH, CH), BF16),
            s((9, 3, CH, CH), BF16),
            s((4, 3, 2, 2, CH, CH), BF16),
            s((2, 256, 128), F32),
            s((4, 256, CH), F32),
            s((2, 2, 512, 128), F32),
            s((nh * nw, 1, 128), F32),
            s((nt, 1, 128), F32),
            s((2, 1, 128), F32),
            s((nt * nh * nw // 2, 1, 128), F32),
            pltpu.SemaphoreType.DMA((4,)),
            pltpu.SemaphoreType.DMA((3, 14)),
            pltpu.SemaphoreType.DMA((3, 14)),
            pltpu.SemaphoreType.DMA((2, 2)),
            pltpu.SemaphoreType.DMA((2, 2)),
        ],
        compiler_params=pltpu.CompilerParams(
            collective_id=0, has_side_effects=True, vmem_limit_bytes=62 * 2**20
        ),
        name="upblock",
    )(
        latents.reshape(2, 2, 64, CH), row(gain1), row(shift1), k1.reshape(9, 3 * CH, CH), row(bias1),
        row(gain2), row(shift2), k2.reshape(9, 3 * CH, CH), row(bias2), ku.reshape(9, 3, CH, CH), row(bias_up),
    )


def solution(mesh):
    sizes = tuple(mesh.shape[a] for a in AXES)
    in_specs = (P(None, "tm", "ha", "wa", None),) + (P(),) * 10
    return jax.shard_map(
        functools.partial(shards, sizes),
        mesh=mesh,
        in_specs=in_specs,
        out_specs=P(None, "tm", "ha", "wa", None),
        check_vma=False,
    )
```

```python
import functools

import jax
import jax.numpy as jnp
from jax import lax
from jax.experimental import pallas as pl
from jax.experimental.pallas import tpu as pltpu
from jax.sharding import PartitionSpec as P

MESH = pl.DeviceIdType.MESH
AXES = ("tm", "ha", "wa")
GROUP = 8
EPS = 1e-6
F32, BF16 = jnp.float32, jnp.bfloat16
CH = 256


def lanes(shape):
    return lax.broadcasted_iota(jnp.int32, shape, len(shape) - 1)


def group_sum(x):
    lane = lanes(x.shape)
    for s in (1, 2, 4):
        x = x + jnp.where((lane // s) % 2 == 0, pltpu.roll(x, 128 - s, 1), pltpu.roll(x, s, 1))
    return x


def halves(x):
    return jnp.concatenate([x[:, :128], x[:, 128:]], axis=0)


def whole(x, clip):
    return jnp.concatenate([x[clip : clip + 1], x[2 + clip : 3 + clip]], axis=1)


def moments(tile, count):
    sums = jnp.sum(jnp.sum(tile, axis=(0, 1)), axis=1)
    mean = group_sum(halves(sums)) * (1.0 / count)
    centre = jnp.stack([whole(mean, 0), whole(mean, 1)])
    dev = tile - centre[None, None]
    spread = group_sum(halves(jnp.sum(jnp.sum(dev * dev, axis=(0, 1)), axis=1)))
    rows = jnp.concatenate([mean[0:2], spread[0:2], mean[2:4], spread[2:4]], axis=0)
    pick = lanes((8, 128)) % 8 == lax.broadcasted_iota(jnp.int32, (8, 128), 0)
    return jnp.sum(jnp.where(pick, rows, 0.0), axis=0, keepdims=True)


def merge(rows, count):
    n = rows.shape[0]
    total = jnp.sum(rows, axis=0)
    mean = total * (1.0 / n)
    dev = rows - mean[None]
    apart = jnp.sum(dev * dev, axis=0)
    return jnp.where(lanes((1, 128)) % 4 < 2, mean, total + float(count) * pltpu.roll(apart, 2, 1))


def spread_out(row, total):
    pick = lanes((8, 128)) % 8 == lax.broadcasted_iota(jnp.int32, (8, 128), 0)
    v = group_sum(jnp.where(pick, row, 0.0))
    mean = [jnp.concatenate([v[c : c + 1], v[4 + c : 5 + c]], axis=1) for c in (0, 1)]
    m2 = [jnp.concatenate([v[2 + c : 3 + c], v[6 + c : 7 + c]], axis=1) for c in (0, 1)]
    return mean, [lax.rsqrt(m * (1.0 / total) + EPS) for m in m2]


def silu(u):
    return u * (0.5 + 0.5 * jnp.tanh(0.5 * u))


def body(sizes, lat, gain1, shift1, k1, bias1, gain2, shift2, k2, bias2, ku, bias_up, out,
         xv, cb, sl, sx, xr, cp, ss, sf, ab, k1v, k2v, kuv, kuc, fbuf, acc, ob, g1, g2, g3, g4, g5, g6,
         lsem, ssem, rsem, gsend, grecv):
    nt, nh, nw = sizes
    it, ih, iw = (lax.axis_index(a) for a in AXES)
    core = lax.rem(ih, 2)

    def at(dt, dh, dw):
        if dh is None:
            return (it, ih + 1 - 2 * lax.rem(ih, 2), iw)
        dt = dt % nt if isinstance(dt, int) else dt
        return (lax.rem(it + dt, nt), lax.rem(ih + dh % nh, nh), lax.rem(iw + dw % nw, nw))

    def ring(d, n):
        return min(d, n - d)

    plane = sorted(
        [(0, a, b) for a in range(nh) for b in range(nw) if a or b],
        key=lambda o: -(ring(o[1], nh) + 2 * ring(o[2], nw)),
    )
    line = sorted([(a, 0, 0) for a in range(1, nt)], key=lambda o: -ring(o[0], nt))

    pair = [(0, None, 0)]
    chips = sorted(
        [(a, 2 * b, c) for a in range(nt // 2) for b in range(nh // 2) for c in range(nw) if a or b or c],
        key=lambda o: -(max(ring(o[0], nt), nt // 2 - o[0]) + ring(o[1], nh) // 2 + ring(o[2], nw)),
    )

    loads = [
        pltpu.make_async_copy(s, d, lsem.at[i])
        for i, (s, d) in enumerate(((lat, xv), (k1, k1v), (ku, kuv), (k2, k2v)))
    ]
    loads[0].start()
    barrier = pltpu.get_barrier_semaphore()
    for o in plane + line:
        pl.semaphore_signal(barrier, inc=1, device_id=at(*o), device_id_type=MESH)
    for c in loads[1:]:
        c.start()

    sends = []

    def send(e, slot, src, dst, offset):
        c = pltpu.make_async_remote_copy(
            src_ref=src, dst_ref=dst, send_sem=ssem.at[e, slot], recv_sem=rsem.at[e, slot],
            device_id=at(*offset), device_id_type=MESH)
        c.start()
        sends.append(c)
        return c

    def columns(e, t0, t1):
        for half in (0, 1):
            for side in (0, 1):
                column = fbuf[half, pl.ds(128 * t0 + 7 * side, 16 * (t1 - t0), stride=8), :]
                ss[e, side, pl.ds(16 * t0, 16 * (t1 - t0)), pl.ds(half * 128, 128)] = column.astype(BF16)

    def corners(e):
        for half in (0, 1):
            sides = [fbuf[half, pl.ds(7 * side, 32, stride=8), :] for side in (0, 1)]
            parts = []
            for h in (0, 14):
                for side in sides:
                    parts += [side[h : h + 2], side[16 + h : 18 + h]]
            sx[e, :, pl.ds(half * 128, 128)] = jnp.concatenate(parts, axis=0).astype(BF16)

    def rows_out(e, t0, t1, slot):
        own = pl.ds(2 + t0, t1 - t0)
        return [
            send(e, slot, cb.at[e, own, 1], cb.at[e, own, 9], (0, -1, 0)),
            send(e, slot + 1, cb.at[e, own, 8], cb.at[e, own, 0], (0, 1, 0)),
        ]

    def columns_out(e, t0, t1, slot):
        part = pl.ds(16 * t0, 16 * (t1 - t0))
        return [
            send(e, slot, ss.at[e, 0, part], sl.at[e, 1, 1, part], (0, 0, -1)),
            send(e, slot + 1, ss.at[e, 1, part], sl.at[e, 1, 0, part], (0, 0, 1)),
        ]

    def corners_out(e):
        return [
            send(e, 4 + 2 * a + b, sx.at[e], xr.at[e, 2 * a + b], (0, 2 * a - 1, 2 * b - 1))
            for a in (0, 1)
            for b in (0, 1)
        ]

    def frames_on(e, t0, t1, slot):
        rows = pl.ds(1, 8)
        return [send(e, slot, cb.at[e, pl.ds(2 + t0, t1 - t0), rows], cb.at[e, pl.ds(t0, t1 - t0), rows], (1, 0, 0))]

    def rows_on(e, t0, t1, slot, arrivals):
        for c in arrivals:
            c.wait_recv()
        return [
            send(e, slot + k, cb.at[e, pl.ds(2 + t0, t1 - t0), h], cb.at[e, pl.ds(t0, t1 - t0), h], (1, 0, 0))
            for k, h in enumerate((0, 9))
        ]

    def columns_on(e, t0, t1, slot, arrivals):
        for c in arrivals:
            c.wait_recv()
        part = pl.ds(16 * t0, 16 * (t1 - t0))
        return [send(e, slot + k, sl.at[e, 1, k, part], sl.at[e, 0, k, part], (1, 0, 0)) for k in (0, 1)]

    def corners_on(e, arrivals):
        for c in arrivals:
            c.wait_recv()
        block = lax.broadcasted_iota(jnp.int32, (16, CH), 0) // 4
        tiles = [xr[e, d].astype(F32) for d in range(4)]
        picked = jnp.where(
            block == 0, tiles[0], jnp.where(block == 1, tiles[1], jnp.where(block == 2, tiles[2], tiles[3]))
        )
        cp[e, 1] = picked.astype(BF16)
        return [send(e, 12, cp.at[e, 1], cp.at[e, 0], (1, 0, 0))]

    def rims_out(e):
        rows = rows_out(e, 0, 2, 0)
        tile = frames_on(e, 0, 2, 8)
        columns(e, 0, 2)
        cols = columns_out(e, 0, 2, 2)
        corners(e)
        return tile, (rows, cols, corners_out(e))

    def rims_on(e, near):
        return rows_on(e, 0, 2, 9, near[0]) + columns_on(e, 0, 2, 13, near[1]) + corners_on(e, near[2])

    def gather(e, phase, buf, row, offsets):
        buf[0] = row
        for slot, o in enumerate(offsets):
            pltpu.make_async_remote_copy(
                src_ref=buf.at[0], dst_ref=buf.at[1 + slot], send_sem=gsend.at[e, phase],
                recv_sem=grecv.at[e, phase], device_id=at(*o), device_id_type=MESH).start()

    def gathered(e, phase, buf, offsets):
        peers = buf.at[pl.ds(1, len(offsets))]
        c = pltpu.make_async_remote_copy(
            src_ref=peers, dst_ref=peers, send_sem=gsend.at[e, phase], recv_sem=grecv.at[e, phase],
            device_id=at(1, 0, 0), device_id_type=MESH)
        c.wait_recv()
        sends.append(c)
        return buf[...]

    def fill(e, frames, norm):
        lo, hi = frames
        pairs = [p for p in (0, 1) if lo <= 2 * p < hi]
        if norm is not None:
            mean, scale, shift = norm
            parity = lax.broadcasted_iota(jnp.int32, (8, CH), 0) % 2 == 0
            mean8 = jnp.where(parity, mean[0], mean[1])
            scale8 = jnp.where(parity, scale[0], scale[1])
            mean2, scale2 = jnp.stack(mean), jnp.stack(scale)

        def act8(x):
            return x if norm is None else silu((x - mean8) * scale8 + shift)

        for p in pairs:
            here = (it > 0) if p == 0 else (it >= 0)
            for side in (0, 1):
                there = jnp.logical_and(here, (iw > 0) if side == 0 else (iw < nw - 1))
                v = act8(sl[e, p, side].astype(F32).reshape(4, 8, CH))
                v = jnp.where(there, v, 0.0).reshape(2, 16, CH)
                for t in (0, 1):
                    sf[side, 2 * p + t, pl.ds(2, 16), :] = v[t]
            v = act8(cp[e, p].astype(F32).reshape(2, 8, CH)).reshape(16, CH)
            for k in range(4):
                above, side = k >= 2, 0 if k % 2 == 1 else 1
                there = jnp.logical_and(here, (ih > 0) if above else (ih < nh - 1))
                there = jnp.logical_and(there, (iw > 0) if side == 0 else (iw < nw - 1))
                w = jnp.where(there, v[4 * k : 4 * k + 4], 0.0)
                for t in (0, 1):
                    sf[side, 2 * p + t, pl.ds(0 if above else 18, 2), :] = w[2 * t : 2 * t + 2]

        sub = lax.broadcasted_iota(jnp.int32, (2, 8, CH), 1)

        for n in range(10 * lo, 10 * hi):
            t, h = n // 10, n % 10
            there = None if t >= 2 else it > 0
            if h in (0, 9):
                row = (ih > 0) if h == 0 else (ih < nh - 1)
                there = row if there is None else jnp.logical_and(there, row)
            x = cb[e, t, h].astype(F32).reshape(2, 8, CH)
            if norm is not None:
                x = silu((x - mean2) * scale2 + shift[None])
            if there is not None:
                x = jnp.where(there, x, 0.0)
            rims = [
                jnp.stack([sf[side, t, pl.ds(2 * h + c, 1), :] for c in (0, 1)])
                for side in (0, 1)
            ]
            before = jnp.where(sub == 0, rims[0], pltpu.roll(x, 1, 1))
            after = jnp.where(sub == 7, rims[1], pltpu.roll(x, 7, 1))
            for k, v in enumerate((before, x, after)):
                ab[t, h, :, pl.ds(k * CH, CH)] = v.reshape(16, CH).astype(BF16)

    def conv(kv, t0, t1):
        total = None
        for i in range(3):
            for j in range(3):
                part = jnp.dot(
                    ab[i + t0 : i + t1, j : j + 8].reshape(128 * (t1 - t0), 3 * CH), kv[3 * i + j], preferred_element_type=F32
                )
                total = part if total is None else total + part
        return total

    def keep(e, value, t0, t1):
        cb[e, 2 + t0 : 2 + t1, 1:9] = value.reshape(t1 - t0, 8, 16, CH).astype(BF16)
        fbuf[0, 128 * t0 : 128 * t1] = value[:, :128]
        fbuf[1, 128 * t0 : 128 * t1] = value[:, 128:]

    def fold():
        def step(n, _):
            t, rows = n // 16, pl.ds(pl.multiple_of((n % 16) * 16, 16), 16)
            cols = []
            for i in range(3):
                k = [kuv[t * 3 + i, j, rows, :].astype(F32) for j in range(3)]
                cols.append((k[0], k[1] + k[2], k[0] + k[1], k[2]))
            for c in range(4):
                v = [cols[i][c] for i in range(3)]
                for r, w in enumerate((v[0], v[1] + v[2], v[0] + v[1], v[2])):
                    kuc[(r // 2) * 2 + c // 2, t, r % 2, c % 2, rows, :] = w.astype(BF16)
            return 0

        lax.fori_loop(0, 48, step, 0)

    cells = 2 * 8 * 8
    total = cells * GROUP * nt * nh * nw
    loads[0].wait()
    x = jnp.stack([xv[c].astype(F32).reshape(2, 8, 8, CH) for c in (0, 1)], axis=2)
    row = moments(x, cells * GROUP)
    keep(0, x.reshape(256, CH), 0, 2)
    pl.semaphore_wait(barrier, len(plane) + len(line))
    gather(0, 0, g1, row, plane)
    onward, near = rims_out(0)
    row = merge(gathered(0, 0, g1, plane), cells * GROUP)
    gather(0, 1, g2, row, line)
    onward += rims_on(0, near)
    loads[2].wait()
    fold()
    row = merge(gathered(0, 1, g2, line), cells * GROUP * nh * nw)
    mean, rstd = spread_out(row, total)
    for c in onward:
        c.wait_recv()
    fill(0, (0, 4), (mean, [r * gain1[...] for r in rstd], shift1[...]))
    loads[1].wait()
    hidden = (conv(k1v, 0, 2) + bias1[...]).astype(BF16).astype(F32)

    row = moments(hidden.reshape(2, 8, 2, 8, CH), cells * GROUP)
    gather(1, 0, g3, row, pair)
    keep(1, hidden, 0, 2)
    onward, near = rims_out(1)
    row = merge(gathered(1, 0, g3, pair), cells * GROUP)
    g5[0] = row
    far = pltpu.make_async_remote_copy(
        src_ref=g5.at[0], dst_ref=g4.at[0], send_sem=gsend.at[1, 2], recv_sem=grecv.at[1, 2],
        device_id=at(nt // 2, 0, 0), device_id_type=MESH)

    @pl.when(core == 0)
    def _():
        g4[0] = row

    @pl.when(core == 1)
    def _():
        far.start()

    for slot, o in enumerate(chips):
        pltpu.make_async_remote_copy(
            src_ref=g5.at[0], dst_ref=g4.at[1 + slot], send_sem=gsend.at[1, 1], recv_sem=grecv.at[1, 1],
            device_id=at(o[0] + nt // 2 * core, o[1], o[2]), device_id_type=MESH).start()
    onward += rims_on(1, near)

    @pl.when(core == 1)
    def _():
        far.wait_recv()
        far.wait_send()

    row = merge(gathered(1, 1, g4, chips), cells * GROUP * 2)
    gather(1, 3, g6, row, pair)
    row = merge(gathered(1, 3, g6, pair), cells * GROUP * nt * nh * nw // 2)
    mean, rstd = spread_out(row, total)
    for c in onward:
        c.wait_recv()
    fill(1, (0, 4), (mean, [r * gain2[...] for r in rstd], shift2[...]))
    loads[3].wait()
    onward, near = [], []
    for t in (0, 1):
        skip = cb[0, 2 + t, 1:9].astype(F32).reshape(128, CH)
        residual = (conv(k2v, t, t + 1) + bias2[...] + skip).astype(BF16).astype(F32)
        keep(2, residual, t, t + 1)
        onward += frames_on(2, t, t + 1, 8 + 13 * t)
        near.append(rows_out(2, t, t + 1, 16 * t))
        columns(2, t, t + 1)
        near.append(columns_out(2, t, t + 1, 2 + 16 * t))
    corners(2)
    near.append(corners_out(2))
    onward += rows_on(2, 0, 1, 9, near[0]) + columns_on(2, 0, 1, 13, near[1])
    onward += rows_on(2, 1, 2, 22, near[2]) + columns_on(2, 1, 2, 24, near[3])
    onward += corners_on(2, near[4])
    fill(2, (2, 4), None)
    up = bias_up[...]

    def window(t0, t1, a, b, r):
        return ab[t0:t1, a + r : a + r + 8, :, b * CH : (b + 2) * CH].reshape(128 * (t1 - t0), 2 * CH)

    def weight(a, b, i, r):
        return kuc[2 * a + b, i, r].reshape(2 * CH, CH)

    for a in (0, 1):
        for b in (0, 1):
            both = sum(jnp.dot(window(2, 4, a, b, r), weight(a, b, 2, r), preferred_element_type=F32) for r in (0, 1))
            late = sum(jnp.dot(window(2, 3, a, b, r), weight(a, b, 1, r), preferred_element_type=F32) for r in (0, 1))
            acc[2 * a + b, 0:128] = both[0:128] + up
            acc[2 * a + b, 128:256] = both[128:256] + late + up
    for c in onward:
        c.wait_recv()
    fill(2, (0, 2), None)
    for a in (0, 1):
        for b in (0, 1):
            both = sum(jnp.dot(window(0, 2, a, b, r), weight(a, b, 0, r), preferred_element_type=F32) for r in (0, 1))
            early = sum(jnp.dot(window(1, 2, a, b, r), weight(a, b, 1, r), preferred_element_type=F32) for r in (0, 1))
            done = [both[0:128] + early + acc[2 * a + b, 0:128], both[128:256] + acc[2 * a + b, 128:256]]
            for t in (0, 1):
                for half in (0, 1):
                    ob[a, half, pl.ds(256 * t + b, 128, stride=2), :] = done[t][:, half * 128 : half * 128 + 128]
        for n in range(32):
            t, h, c = n // 16, (n // 2) % 8, n % 2
            for half in (0, 1):
                out[c, t, 2 * h + a, :, pl.ds(half * 128, 128)] = ob[a, half, pl.ds(16 * n, 16), :].astype(BF16)
    for c in sends:
        c.wait_send()


def shards(sizes, latents, gain1, shift1, k1, bias1, gain2, shift2, k2, bias2, ku, bias_up):
    nt, nh, nw = sizes
    row = lambda v: v.reshape(1, CH)
    vmem = pl.BlockSpec(memory_space=pltpu.VMEM)
    hbm = pl.BlockSpec(memory_space=pl.ANY)
    s = pltpu.VMEM
    return pl.pallas_call(
        functools.partial(body, sizes),
        out_shape=pltpu.VMEM((2, 2, 16, 16, CH), BF16),
        in_specs=[hbm, vmem, vmem, hbm, vmem, vmem, vmem, hbm, vmem, hbm, vmem],
        out_specs=vmem,
        scratch_shapes=[
            s((2, 2, 64, CH), BF16),
            s((3, 4, 10, 16, CH), BF16),
            s((3, 2, 2, 32, CH), BF16),
            s((3, 16, CH), BF16),
            s((3, 4, 16, CH), BF16),
            s((3, 2, 16, CH), BF16),
            s((3, 2, 32, CH), BF16),
            s((2, 4, 20, CH), F32),
            s((4, 10, 16, 3 * CH), BF16),
            s((9, 3 * CH, CH), BF16),
            s((9, 3 * CH, CH), BF16),
            s((9, 3, CH, CH), BF16),
            s((4, 3, 2, 2, CH, CH), BF16),
            s((2, 256, 128), F32),
            s((4, 256, CH), F32),
            s((2, 2, 512, 128), F32),
            s((nh * nw, 1, 128), F32),
            s((nt, 1, 128), F32),
            s((2, 1, 128), F32),
            s((nt * nh * nw // 4, 1, 128), F32),
            s((1, 1, 128), F32),
            s((2, 1, 128), F32),
            pltpu.SemaphoreType.DMA((4,)),
            pltpu.SemaphoreType.DMA((3, 26)),
            pltpu.SemaphoreType.DMA((3, 26)),
            pltpu.SemaphoreType.DMA((2, 4)),
            pltpu.SemaphoreType.DMA((2, 4)),
        ],
        compiler_params=pltpu.CompilerParams(
            collective_id=0, has_side_effects=True, vmem_limit_bytes=62 * 2**20
        ),
        name="upblock",
    )(
        latents.reshape(2, 2, 64, CH), row(gain1), row(shift1), k1.reshape(9, 3 * CH, CH), row(bias1),
        row(gain2), row(shift2), k2.reshape(9, 3 * CH, CH), row(bias2), ku.reshape(9, 3, CH, CH), row(bias_up),
    )


def solution(mesh):
    sizes = tuple(mesh.shape[a] for a in AXES)
    in_specs = (P(None, "tm", "ha", "wa", None),) + (P(),) * 10
    return jax.shard_map(
        functools.partial(shards, sizes),
        mesh=mesh,
        in_specs=in_specs,
        out_specs=P(None, "tm", "ha", "wa", None),
        check_vma=False,
    )
```

```python
import functools

import jax
import jax.numpy as jnp
from jax import lax
from jax.experimental import pallas as pl
from jax.experimental.pallas import tpu as pltpu
from jax.sharding import PartitionSpec as P

MESH = pl.DeviceIdType.MESH
AXES = ("tm", "ha", "wa")
GROUP = 8
EPS = 1e-6
F32, BF16 = jnp.float32, jnp.bfloat16
CH = 256


def lanes(shape):
    return lax.broadcasted_iota(jnp.int32, shape, len(shape) - 1)


def group_sum(x):
    lane = lanes(x.shape)
    for s in (1, 2, 4):
        x = x + jnp.where((lane // s) % 2 == 0, pltpu.roll(x, 128 - s, 1), pltpu.roll(x, s, 1))
    return x


def halves(x):
    return jnp.concatenate([x[:, :128], x[:, 128:]], axis=0)


def whole(x, clip):
    return jnp.concatenate([x[clip : clip + 1], x[2 + clip : 3 + clip]], axis=1)


def moments(tile, count):
    sums = jnp.sum(jnp.sum(tile, axis=(0, 1)), axis=1)
    mean = group_sum(halves(sums)) * (1.0 / count)
    centre = jnp.stack([whole(mean, 0), whole(mean, 1)])
    dev = tile - centre[None, None]
    spread = group_sum(halves(jnp.sum(jnp.sum(dev * dev, axis=(0, 1)), axis=1)))
    rows = jnp.concatenate([mean[0:2], spread[0:2], mean[2:4], spread[2:4]], axis=0)
    pick = lanes((8, 128)) % 8 == lax.broadcasted_iota(jnp.int32, (8, 128), 0)
    return jnp.sum(jnp.where(pick, rows, 0.0), axis=0, keepdims=True)


def merge(rows, count):
    n = rows.shape[0]
    total = jnp.sum(rows, axis=0)
    mean = total * (1.0 / n)
    dev = rows - mean[None]
    apart = jnp.sum(dev * dev, axis=0)
    return jnp.where(lanes((1, 128)) % 4 < 2, mean, total + float(count) * pltpu.roll(apart, 2, 1))


def spread_out(row, total):
    pick = lanes((8, 128)) % 8 == lax.broadcasted_iota(jnp.int32, (8, 128), 0)
    v = group_sum(jnp.where(pick, row, 0.0))
    mean = [jnp.concatenate([v[c : c + 1], v[4 + c : 5 + c]], axis=1) for c in (0, 1)]
    m2 = [jnp.concatenate([v[2 + c : 3 + c], v[6 + c : 7 + c]], axis=1) for c in (0, 1)]
    return mean, [lax.rsqrt(m * (1.0 / total) + EPS) for m in m2]


def silu(u):
    return u * (0.5 + 0.5 * jnp.tanh(0.5 * u))


def body(sizes, lat, gain1, shift1, k1, bias1, gain2, shift2, k2, bias2, ku, bias_up, out,
         xv, cb, sl, sx, xr, cp, ss, sf, ab, k1v, k2v, kuv, kuc, fbuf, acc, ob, g1, g2, g3, g4, g5, g6,
         lsem, ssem, rsem, gsend, grecv):
    nt, nh, nw = sizes
    it, ih, iw = (lax.axis_index(a) for a in AXES)
    core = lax.bitwise_and(ih, 1)

    def turn(index, n):
        return lax.bitwise_and(index, n - 1) if n & (n - 1) == 0 else lax.rem(index, n)

    places = [[turn(i + d, n) if d else i for d in range(n)] for i, n in ((it, nt), (ih, nh), (iw, nw))]
    halfway = [turn(i + nt // 2 * core, nt) for i in places[0]]

    def at(dt, dh, dw):
        if dh is None:
            return (it, ih + 1 - 2 * core, iw)
        return (places[0][dt % nt], places[1][dh % nh], places[2][dw % nw])

    def ring(d, n):
        return min(d, n - d)

    plane = sorted(
        [(0, a, b) for a in range(nh) for b in range(nw) if a or b],
        key=lambda o: -(ring(o[1], nh) + 2 * ring(o[2], nw)),
    )
    line = sorted([(a, 0, 0) for a in range(1, nt)], key=lambda o: -ring(o[0], nt))

    pair = [(0, None, 0)]
    chips = sorted(
        [(a, 2 * b, c) for a in range(nt // 2) for b in range(nh // 2) for c in range(nw) if a or b or c],
        key=lambda o: -(max(ring(o[0], nt), nt // 2 - o[0]) + ring(o[1], nh) // 2 + ring(o[2], nw)),
    )

    loads = [
        pltpu.make_async_copy(s, d, lsem.at[i])
        for i, (s, d) in enumerate(((lat, xv), (k1, k1v), (ku, kuv), (k2, k2v)))
    ]
    loads[0].start()
    barrier = pltpu.get_barrier_semaphore()
    for o in plane + line:
        pl.semaphore_signal(barrier, inc=1, device_id=at(*o), device_id_type=MESH)
    for c in loads[1:]:
        c.start()

    sends = []

    def send(e, slot, src, dst, offset):
        c = pltpu.make_async_remote_copy(
            src_ref=src, dst_ref=dst, send_sem=ssem.at[e, slot], recv_sem=rsem.at[e, slot],
            device_id=at(*offset), device_id_type=MESH)
        c.start()
        sends.append(c)
        return c

    def columns(e, t0, t1):
        for half in (0, 1):
            for side in (0, 1):
                column = fbuf[half, pl.ds(128 * t0 + 7 * side, 16 * (t1 - t0), stride=8), :]
                ss[e, side, pl.ds(16 * t0, 16 * (t1 - t0)), pl.ds(half * 128, 128)] = column.astype(BF16)

    def corners(e):
        for half in (0, 1):
            sides = [fbuf[half, pl.ds(7 * side, 32, stride=8), :] for side in (0, 1)]
            parts = []
            for h in (0, 14):
                for side in sides:
                    parts += [side[h : h + 2], side[16 + h : 18 + h]]
            sx[e, :, pl.ds(half * 128, 128)] = jnp.concatenate(parts, axis=0).astype(BF16)

    def rows_out(e, t0, t1, slot):
        own = pl.ds(2 + t0, t1 - t0)
        return [
            send(e, slot, cb.at[e, own, 1], cb.at[e, own, 9], (0, -1, 0)),
            send(e, slot + 1, cb.at[e, own, 8], cb.at[e, own, 0], (0, 1, 0)),
        ]

    def columns_out(e, t0, t1, slot):
        part = pl.ds(16 * t0, 16 * (t1 - t0))
        return [
            send(e, slot, ss.at[e, 0, part], sl.at[e, 1, 1, part], (0, 0, -1)),
            send(e, slot + 1, ss.at[e, 1, part], sl.at[e, 1, 0, part], (0, 0, 1)),
        ]

    def corners_out(e):
        return [
            send(e, 4 + 2 * a + b, sx.at[e], xr.at[e, 2 * a + b], (0, 2 * a - 1, 2 * b - 1))
            for a in (0, 1)
            for b in (0, 1)
        ]

    def frames_on(e, t0, t1, slot):
        rows = pl.ds(1, 8)
        return [send(e, slot, cb.at[e, pl.ds(2 + t0, t1 - t0), rows], cb.at[e, pl.ds(t0, t1 - t0), rows], (1, 0, 0))]

    def rows_on(e, t0, t1, slot, arrivals):
        for c in arrivals:
            c.wait_recv()
        return [
            send(e, slot + k, cb.at[e, pl.ds(2 + t0, t1 - t0), h], cb.at[e, pl.ds(t0, t1 - t0), h], (1, 0, 0))
            for k, h in enumerate((0, 9))
        ]

    def columns_on(e, t0, t1, slot, arrivals):
        for c in arrivals:
            c.wait_recv()
        part = pl.ds(16 * t0, 16 * (t1 - t0))
        return [send(e, slot + k, sl.at[e, 1, k, part], sl.at[e, 0, k, part], (1, 0, 0)) for k in (0, 1)]

    def corners_on(e, arrivals):
        for c in arrivals:
            c.wait_recv()
        block = lax.broadcasted_iota(jnp.int32, (16, CH), 0) // 4
        tiles = [xr[e, d].astype(F32) for d in range(4)]
        picked = jnp.where(
            block == 0, tiles[0], jnp.where(block == 1, tiles[1], jnp.where(block == 2, tiles[2], tiles[3]))
        )
        cp[e, 1] = picked.astype(BF16)
        return [send(e, 12, cp.at[e, 1], cp.at[e, 0], (1, 0, 0))]

    def rims_out(e, tile_now=True):
        rows = rows_out(e, 0, 2, 0)
        tile = frames_on(e, 0, 2, 8) if tile_now else []
        columns(e, 0, 2)
        cols = columns_out(e, 0, 2, 2)
        corners(e)
        return tile, (rows, cols, corners_out(e))

    def rims_on(e, near):
        return rows_on(e, 0, 2, 9, near[0]) + columns_on(e, 0, 2, 13, near[1]) + corners_on(e, near[2])

    def gather(e, phase, buf, row, offsets):
        buf[0] = row
        for slot, o in enumerate(offsets):
            pltpu.make_async_remote_copy(
                src_ref=buf.at[0], dst_ref=buf.at[1 + slot], send_sem=gsend.at[e, phase],
                recv_sem=grecv.at[e, phase], device_id=at(*o), device_id_type=MESH).start()

    def gathered(e, phase, buf, offsets):
        peers = buf.at[pl.ds(1, len(offsets))]
        c = pltpu.make_async_remote_copy(
            src_ref=peers, dst_ref=peers, send_sem=gsend.at[e, phase], recv_sem=grecv.at[e, phase],
            device_id=at(1, 0, 0), device_id_type=MESH)
        c.wait_recv()
        sends.append(c)
        return buf[...]

    def fill(e, frames, norm):
        lo, hi = frames
        if norm is not None:
            mean, scale, shift = norm
            parity = lax.broadcasted_iota(jnp.int32, (8, CH), 0) % 2 == 0
            mean8 = jnp.where(parity, mean[0], mean[1])
            scale8 = jnp.where(parity, scale[0], scale[1])
            mean2, scale2 = jnp.stack(mean), jnp.stack(scale)

        def act8(x):
            return x if norm is None else silu((x - mean8) * scale8 + shift)

        for t in range(lo, hi):
            p, tt = t // 2, t % 2
            here = (it > 0) if p == 0 else (it >= 0)
            for side in (0, 1):
                there = jnp.logical_and(here, (iw > 0) if side == 0 else (iw < nw - 1))
                v = act8(sl[e, p, side, pl.ds(16 * tt, 16)].astype(F32).reshape(2, 8, CH))
                sf[side, t, pl.ds(2, 16), :] = jnp.where(there, v, 0.0).reshape(16, CH)
            v = act8(cp[e, p].astype(F32).reshape(2, 8, CH)).reshape(16, CH)
            for k in range(4):
                above, side = k >= 2, 0 if k % 2 == 1 else 1
                there = jnp.logical_and(here, (ih > 0) if above else (ih < nh - 1))
                there = jnp.logical_and(there, (iw > 0) if side == 0 else (iw < nw - 1))
                at_k = 4 * k + 2 * tt
                sf[side, t, pl.ds(0 if above else 18, 2), :] = jnp.where(there, v[at_k : at_k + 2], 0.0)

        sub = lax.broadcasted_iota(jnp.int32, (2, 8, CH), 1)

        for n in range(10 * lo, 10 * hi):
            t, h = n // 10, n % 10
            there = None if t >= 2 else it > 0
            if h in (0, 9):
                row = (ih > 0) if h == 0 else (ih < nh - 1)
                there = row if there is None else jnp.logical_and(there, row)
            x = cb[e, t, h].astype(F32).reshape(2, 8, CH)
            if norm is not None:
                x = silu((x - mean2) * scale2 + shift[None])
            if there is not None:
                x = jnp.where(there, x, 0.0)
            rims = [
                jnp.stack([sf[side, t, pl.ds(2 * h + c, 1), :] for c in (0, 1)])
                for side in (0, 1)
            ]
            before = jnp.where(sub == 0, rims[0], pltpu.roll(x, 1, 1))
            after = jnp.where(sub == 7, rims[1], pltpu.roll(x, 7, 1))
            for k, v in enumerate((before, x, after)):
                ab[t, h, :, pl.ds(k * CH, CH)] = v.reshape(16, CH).astype(BF16)

    def conv(kv, t0, t1):
        total = None
        for i in range(3):
            for j in range(3):
                part = jnp.dot(
                    ab[i + t0 : i + t1, j : j + 8].reshape(128 * (t1 - t0), 3 * CH), kv[3 * i + j], preferred_element_type=F32
                )
                total = part if total is None else total + part
        return total

    def keep(e, value, t0, t1):
        cb[e, 2 + t0 : 2 + t1, 1:9] = value.reshape(t1 - t0, 8, 16, CH).astype(BF16)
        fbuf[0, 128 * t0 : 128 * t1] = value[:, :128]
        fbuf[1, 128 * t0 : 128 * t1] = value[:, 128:]

    def fold():
        def step(n, _):
            t, rows = n // 16, pl.ds(pl.multiple_of((n % 16) * 16, 16), 16)
            cols = []
            for i in range(3):
                k = [kuv[t * 3 + i, j, rows, :].astype(F32) for j in range(3)]
                cols.append((k[0], k[1] + k[2], k[0] + k[1], k[2]))
            for c in range(4):
                v = [cols[i][c] for i in range(3)]
                for r, w in enumerate((v[0], v[1] + v[2], v[0] + v[1], v[2])):
                    kuc[(r // 2) * 2 + c // 2, t, r % 2, c % 2, rows, :] = w.astype(BF16)
            return 0

        lax.fori_loop(0, 48, step, 0)

    cells = 2 * 8 * 8
    total = cells * GROUP * nt * nh * nw
    loads[0].wait()
    x = jnp.stack([xv[c].astype(F32).reshape(2, 8, 8, CH) for c in (0, 1)], axis=2)
    row = moments(x, cells * GROUP)
    keep(0, x.reshape(256, CH), 0, 2)
    pl.semaphore_wait(barrier, len(plane) + len(line))
    gather(0, 0, g1, row, plane)
    onward, near = rims_out(0)
    row = merge(gathered(0, 0, g1, plane), cells * GROUP)
    gather(0, 1, g2, row, line)
    onward += rims_on(0, near)
    loads[2].wait()
    fold()
    row = merge(gathered(0, 1, g2, line), cells * GROUP * nh * nw)
    mean, rstd = spread_out(row, total)
    for c in onward:
        c.wait_recv()
    fill(0, (0, 4), (mean, [r * gain1[...] for r in rstd], shift1[...]))
    loads[1].wait()
    hidden = (conv(k1v, 0, 2) + bias1[...]).astype(BF16).astype(F32)

    row = moments(hidden.reshape(2, 8, 2, 8, CH), cells * GROUP)
    gather(1, 0, g3, row, pair)
    keep(1, hidden, 0, 2)
    onward, near = rims_out(1, False)
    row = merge(gathered(1, 0, g3, pair), cells * GROUP)
    g5[0] = row
    far = pltpu.make_async_remote_copy(
        src_ref=g5.at[0], dst_ref=g4.at[0], send_sem=gsend.at[1, 2], recv_sem=grecv.at[1, 2],
        device_id=at(nt // 2, 0, 0), device_id_type=MESH)

    @pl.when(core == 0)
    def _():
        g4[0] = row

    @pl.when(core == 1)
    def _():
        far.start()

    for slot, o in enumerate(chips):
        pltpu.make_async_remote_copy(
            src_ref=g5.at[0], dst_ref=g4.at[1 + slot], send_sem=gsend.at[1, 1], recv_sem=grecv.at[1, 1],
            device_id=(halfway[o[0]],) + at(*o)[1:], device_id_type=MESH).start()
    onward += frames_on(1, 0, 2, 8) + rims_on(1, near)

    @pl.when(core == 1)
    def _():
        far.wait_recv()
        far.wait_send()

    row = merge(gathered(1, 1, g4, chips), cells * GROUP * 2)
    gather(1, 3, g6, row, pair)
    row = merge(gathered(1, 3, g6, pair), cells * GROUP * nt * nh * nw // 2)
    mean, rstd = spread_out(row, total)
    for c in onward:
        c.wait_recv()
    fill(1, (0, 4), (mean, [r * gain2[...] for r in rstd], shift2[...]))
    loads[3].wait()
    earlier = list(sends)
    sends.clear()
    onward, near = [], []
    for t in (0, 1):
        skip = cb[0, 2 + t, 1:9].astype(F32).reshape(128, CH)
        residual = (conv(k2v, t, t + 1) + bias2[...] + skip).astype(BF16).astype(F32)
        keep(2, residual, t, t + 1)
        onward += frames_on(2, t, t + 1, 8 + 13 * t)
        near.append(rows_out(2, t, t + 1, 16 * t))
        columns(2, t, t + 1)
        near.append(columns_out(2, t, t + 1, 2 + 16 * t))
    corners(2)
    near.append(corners_out(2))
    first = onward[:1] + rows_on(2, 0, 1, 9, near[0]) + columns_on(2, 0, 1, 13, near[1])
    first += corners_on(2, near[4])
    second = onward[1:] + rows_on(2, 1, 2, 22, near[2]) + columns_on(2, 1, 2, 24, near[3])
    fill(2, (2, 4), None)
    up = bias_up[...]

    def window(t0, t1, a, b, r):
        return ab[t0:t1, a + r : a + r + 8, :, b * CH : (b + 2) * CH].reshape(128 * (t1 - t0), 2 * CH)

    def weight(a, b, i, r):
        return kuc[2 * a + b, i, r].reshape(2 * CH, CH)

    for a in (0, 1):
        for b in (0, 1):
            both = sum(jnp.dot(window(2, 4, a, b, r), weight(a, b, 2, r), preferred_element_type=F32) for r in (0, 1))
            late = sum(jnp.dot(window(2, 3, a, b, r), weight(a, b, 1, r), preferred_element_type=F32) for r in (0, 1))
            acc[2 * a + b, 0:128] = both[0:128] + up
            acc[2 * a + b, 128:256] = both[128:256] + late + up
    for c in earlier:
        c.wait_send()
    for c in first:
        c.wait_recv()
    fill(2, (0, 1), None)
    for a in (0, 1):
        for b in (0, 1):
            acc[2 * a + b, 0:128] += sum(
                jnp.dot(window(0, 1, a, b, r), weight(a, b, 0, r), preferred_element_type=F32) for r in (0, 1)
            )
    for c in second:
        c.wait_recv()
    fill(2, (1, 2), None)
    for a in (0, 1):
        for b in (0, 1):
            late, early = (
                sum(jnp.dot(window(1, 2, a, b, r), weight(a, b, i, r), preferred_element_type=F32) for r in (0, 1))
                for i in (0, 1)
            )
            done = [early + acc[2 * a + b, 0:128], late + acc[2 * a + b, 128:256]]
            for t in (0, 1):
                for half in (0, 1):
                    ob[a, half, pl.ds(256 * t + b, 128, stride=2), :] = done[t][:, half * 128 : half * 128 + 128]
        for n in range(32):
            t, h, c = n // 16, (n // 2) % 8, n % 2
            for half in (0, 1):
                out[c, t, 2 * h + a, :, pl.ds(half * 128, 128)] = ob[a, half, pl.ds(16 * n, 16), :].astype(BF16)
    for c in sends:
        c.wait_send()


def shards(sizes, latents, gain1, shift1, k1, bias1, gain2, shift2, k2, bias2, ku, bias_up):
    nt, nh, nw = sizes
    row = lambda v: v.reshape(1, CH)
    vmem = pl.BlockSpec(memory_space=pltpu.VMEM)
    hbm = pl.BlockSpec(memory_space=pl.ANY)
    s = pltpu.VMEM
    return pl.pallas_call(
        functools.partial(body, sizes),
        out_shape=pltpu.VMEM((2, 2, 16, 16, CH), BF16),
        in_specs=[hbm, vmem, vmem, hbm, vmem, vmem, vmem, hbm, vmem, hbm, vmem],
        out_specs=vmem,
        scratch_shapes=[
            s((2, 2, 64, CH), BF16),
            s((3, 4, 10, 16, CH), BF16),
            s((3, 2, 2, 32, CH), BF16),
            s((3, 16, CH), BF16),
            s((3, 4, 16, CH), BF16),
            s((3, 2, 16, CH), BF16),
            s((3, 2, 32, CH), BF16),
            s((2, 4, 20, CH), F32),
            s((4, 10, 16, 3 * CH), BF16),
            s((9, 3 * CH, CH), BF16),
            s((9, 3 * CH, CH), BF16),
            s((9, 3, CH, CH), BF16),
            s((4, 3, 2, 2, CH, CH), BF16),
            s((2, 264, 128), F32),
            s((4, 256, CH), F32),
            s((2, 2, 520, 128), F32),
            s((nh * nw, 1, 128), F32),
            s((nt, 1, 128), F32),
            s((2, 1, 128), F32),
            s((nt * nh * nw // 4, 1, 128), F32),
            s((1, 1, 128), F32),
            s((2, 1, 128), F32),
            pltpu.SemaphoreType.DMA((4,)),
            pltpu.SemaphoreType.DMA((3, 26)),
            pltpu.SemaphoreType.DMA((3, 26)),
            pltpu.SemaphoreType.DMA((2, 4)),
            pltpu.SemaphoreType.DMA((2, 4)),
        ],
        compiler_params=pltpu.CompilerParams(
            collective_id=0, has_side_effects=True, vmem_limit_bytes=62 * 2**20
        ),
        name="upblock",
    )(
        latents.reshape(2, 2, 64, CH), row(gain1), row(shift1), k1.reshape(9, 3 * CH, CH), row(bias1),
        row(gain2), row(shift2), k2.reshape(9, 3 * CH, CH), row(bias2), ku.reshape(9, 3, CH, CH), row(bias_up),
    )


def solution(mesh):
    sizes = tuple(mesh.shape[a] for a in AXES)
    in_specs = (P(None, "tm", "ha", "wa", None),) + (P(),) * 10
    return jax.shard_map(
        functools.partial(shards, sizes),
        mesh=mesh,
        in_specs=in_specs,
        out_specs=P(None, "tm", "ha", "wa", None),
        check_vma=False,
    )
```

```python
import functools

import jax
import jax.numpy as jnp
from jax import lax
from jax.experimental import pallas as pl
from jax.experimental.pallas import tpu as pltpu
from jax.sharding import PartitionSpec as P

MESH = pl.DeviceIdType.MESH
AXES = ("tm", "ha", "wa")
GROUP = 8
EPS = 1e-6
F32, BF16 = jnp.float32, jnp.bfloat16
CH = 256


def lanes(shape):
    return lax.broadcasted_iota(jnp.int32, shape, len(shape) - 1)


def group_sum(x):
    lane = lanes(x.shape)
    for s in (1, 2, 4):
        x = x + jnp.where((lane // s) % 2 == 0, pltpu.roll(x, 128 - s, 1), pltpu.roll(x, s, 1))
    return x


def halves(x):
    return jnp.concatenate([x[:, :128], x[:, 128:]], axis=0)


def whole(x, clip):
    return jnp.concatenate([x[clip : clip + 1], x[2 + clip : 3 + clip]], axis=1)


def moments(tile, count):
    sums = jnp.sum(jnp.sum(tile, axis=(0, 1)), axis=1)
    mean = group_sum(halves(sums)) * (1.0 / count)
    centre = jnp.stack([whole(mean, 0), whole(mean, 1)])
    dev = tile - centre[None, None]
    spread = group_sum(halves(jnp.sum(jnp.sum(dev * dev, axis=(0, 1)), axis=1)))
    rows = jnp.concatenate([mean[0:2], spread[0:2], mean[2:4], spread[2:4]], axis=0)
    pick = lanes((8, 128)) % 8 == lax.broadcasted_iota(jnp.int32, (8, 128), 0)
    return jnp.sum(jnp.where(pick, rows, 0.0), axis=0, keepdims=True)


def merge(rows, count):
    n = rows.shape[0]
    total = jnp.sum(rows, axis=0)
    mean = total * (1.0 / n)
    dev = rows - mean[None]
    apart = jnp.sum(dev * dev, axis=0)
    return jnp.where(lanes((1, 128)) % 4 < 2, mean, total + float(count) * pltpu.roll(apart, 2, 1))


def spread_out(row, total):
    pick = lanes((8, 128)) % 8 == lax.broadcasted_iota(jnp.int32, (8, 128), 0)
    v = group_sum(jnp.where(pick, row, 0.0))
    mean = [jnp.concatenate([v[c : c + 1], v[4 + c : 5 + c]], axis=1) for c in (0, 1)]
    m2 = [jnp.concatenate([v[2 + c : 3 + c], v[6 + c : 7 + c]], axis=1) for c in (0, 1)]
    return mean, [lax.rsqrt(m * (1.0 / total) + EPS) for m in m2]


def silu(u):
    return u * (0.5 + 0.5 * jnp.tanh(0.5 * u))


def body(sizes, lat, gain1, shift1, k1, bias1, gain2, shift2, k2, bias2, ku, bias_up, out,
         xv, cb, sl, sx, xr, cp, ss, sf, ab, k1v, k2v, kuv, kuc, fbuf, acc, ob, g1, g2, g3, g4, g5, g6,
         lsem, ssem, rsem, gsend, grecv):
    nt, nh, nw = sizes
    it, ih, iw = (lax.axis_index(a) for a in AXES)
    core = lax.bitwise_and(ih, 1)

    def turn(index, n):
        return lax.bitwise_and(index, n - 1) if n & (n - 1) == 0 else lax.rem(index, n)

    places = [[turn(i + d, n) if d else i for d in range(n)] for i, n in ((it, nt), (ih, nh), (iw, nw))]
    halfway = [turn(i + nt // 2 * core, nt) for i in places[0]]

    def at(dt, dh, dw):
        if dh is None:
            return (it, ih + 1 - 2 * core, iw)
        return (places[0][dt % nt], places[1][dh % nh], places[2][dw % nw])

    def ring(d, n):
        return min(d, n - d)

    plane = sorted(
        [(0, a, b) for a in range(nh) for b in range(nw) if a or b],
        key=lambda o: -(ring(o[1], nh) + 2 * ring(o[2], nw)),
    )
    line = sorted([(a, 0, 0) for a in range(1, nt)], key=lambda o: -ring(o[0], nt))

    pair = [(0, None, 0)]
    chips = sorted(
        [(a, 2 * b, c) for a in range(nt // 2) for b in range(nh // 2) for c in range(nw) if a or b or c],
        key=lambda o: -(max(ring(o[0], nt), nt // 2 - o[0]) + ring(o[1], nh) // 2 + ring(o[2], nw)),
    )

    loads = [
        pltpu.make_async_copy(s, d, lsem.at[i])
        for i, (s, d) in enumerate(((lat, xv), (k1, k1v), (ku, kuv), (k2, k2v)))
    ]
    loads[0].start()
    barrier = pltpu.get_barrier_semaphore()
    for o in sorted(plane + line, key=lambda o: -(2 * ring(o[0], nt) + ring(o[1], nh) + 2 * ring(o[2], nw))):
        pl.semaphore_signal(barrier, inc=1, device_id=at(*o), device_id_type=MESH)
    for c in loads[1:]:
        c.start()

    sends = []

    def send(e, slot, src, dst, offset):
        c = pltpu.make_async_remote_copy(
            src_ref=src, dst_ref=dst, send_sem=ssem.at[e, slot], recv_sem=rsem.at[e, slot],
            device_id=at(*offset), device_id_type=MESH)
        c.start()
        sends.append(c)
        return c

    def columns(e, t0, t1):
        for half in (0, 1):
            for side in (0, 1):
                column = fbuf[half, pl.ds(128 * t0 + 7 * side, 16 * (t1 - t0), stride=8), :]
                ss[e, side, pl.ds(16 * t0, 16 * (t1 - t0)), pl.ds(half * 128, 128)] = column.astype(BF16)

    def corners(e):
        for half in (0, 1):
            sides = [fbuf[half, pl.ds(7 * side, 32, stride=8), :] for side in (0, 1)]
            parts = []
            for h in (0, 14):
                for side in sides:
                    parts += [side[h : h + 2], side[16 + h : 18 + h]]
            sx[e, :, pl.ds(half * 128, 128)] = jnp.concatenate(parts, axis=0).astype(BF16)

    def rows_out(e, t0, t1, slot):
        own = pl.ds(2 + t0, t1 - t0)
        return [
            send(e, slot, cb.at[e, own, 1], cb.at[e, own, 9], (0, -1, 0)),
            send(e, slot + 1, cb.at[e, own, 8], cb.at[e, own, 0], (0, 1, 0)),
        ]

    def columns_out(e, t0, t1, slot):
        part = pl.ds(16 * t0, 16 * (t1 - t0))
        return [
            send(e, slot, ss.at[e, 0, part], sl.at[e, 1, 1, part], (0, 0, -1)),
            send(e, slot + 1, ss.at[e, 1, part], sl.at[e, 1, 0, part], (0, 0, 1)),
        ]

    def corners_out(e):
        return [
            send(e, 4 + 2 * a + b, sx.at[e], xr.at[e, 2 * a + b], (0, 2 * a - 1, 2 * b - 1))
            for a in (0, 1)
            for b in (0, 1)
        ]

    def frames_on(e, t0, t1, slot):
        rows = pl.ds(1, 8)
        return [send(e, slot, cb.at[e, pl.ds(2 + t0, t1 - t0), rows], cb.at[e, pl.ds(t0, t1 - t0), rows], (1, 0, 0))]

    def rows_on(e, t0, t1, slot, arrivals):
        for c in arrivals:
            c.wait_recv()
        return [
            send(e, slot + k, cb.at[e, pl.ds(2 + t0, t1 - t0), h], cb.at[e, pl.ds(t0, t1 - t0), h], (1, 0, 0))
            for k, h in enumerate((0, 9))
        ]

    def columns_on(e, t0, t1, slot, arrivals):
        for c in arrivals:
            c.wait_recv()
        part = pl.ds(16 * t0, 16 * (t1 - t0))
        return [send(e, slot + k, sl.at[e, 1, k, part], sl.at[e, 0, k, part], (1, 0, 0)) for k in (0, 1)]

    def corners_on(e, arrivals):
        for c in arrivals:
            c.wait_recv()
        block = lax.broadcasted_iota(jnp.int32, (16, CH), 0) // 4
        tiles = [xr[e, d].astype(F32) for d in range(4)]
        picked = jnp.where(
            block == 0, tiles[0], jnp.where(block == 1, tiles[1], jnp.where(block == 2, tiles[2], tiles[3]))
        )
        cp[e, 1] = picked.astype(BF16)
        return [send(e, 12, cp.at[e, 1], cp.at[e, 0], (1, 0, 0))]

    def rims_out(e, tile_now=True):
        rows = rows_out(e, 0, 2, 0)
        tile = frames_on(e, 0, 2, 8) if tile_now else []
        columns(e, 0, 2)
        cols = columns_out(e, 0, 2, 2)
        return tile, rows, cols

    def rims_on(e, near):
        return rows_on(e, 0, 2, 9, near[0]) + columns_on(e, 0, 2, 13, near[1]) + corners_on(e, near[2])

    def gather(e, phase, buf, row, offsets):
        buf[0] = row
        for slot, o in enumerate(offsets):
            pltpu.make_async_remote_copy(
                src_ref=buf.at[0], dst_ref=buf.at[1 + slot], send_sem=gsend.at[e, phase],
                recv_sem=grecv.at[e, phase], device_id=at(*o), device_id_type=MESH).start()

    def gathered(e, phase, buf, offsets):
        peers = buf.at[pl.ds(1, len(offsets))]
        c = pltpu.make_async_remote_copy(
            src_ref=peers, dst_ref=peers, send_sem=gsend.at[e, phase], recv_sem=grecv.at[e, phase],
            device_id=at(1, 0, 0), device_id_type=MESH)
        c.wait_recv()
        sends.append(c)
        return buf[...]

    def fill(e, frames, norm):
        lo, hi = frames
        if norm is not None:
            mean, scale, shift = norm
            parity = lax.broadcasted_iota(jnp.int32, (8, CH), 0) % 2 == 0
            mean8 = jnp.where(parity, mean[0], mean[1])
            scale8 = jnp.where(parity, scale[0], scale[1])
            mean2, scale2 = jnp.stack(mean), jnp.stack(scale)

        def act8(x):
            return x if norm is None else silu((x - mean8) * scale8 + shift)

        for t in range(lo, hi):
            p, tt = t // 2, t % 2
            here = (it > 0) if p == 0 else (it >= 0)
            for side in (0, 1):
                there = jnp.logical_and(here, (iw > 0) if side == 0 else (iw < nw - 1))
                v = act8(sl[e, p, side, pl.ds(16 * tt, 16)].astype(F32).reshape(2, 8, CH))
                sf[side, t, pl.ds(2, 16), :] = jnp.where(there, v, 0.0).reshape(16, CH)
            v = act8(cp[e, p].astype(F32).reshape(2, 8, CH)).reshape(16, CH)
            for k in range(4):
                above, side = k >= 2, 0 if k % 2 == 1 else 1
                there = jnp.logical_and(here, (ih > 0) if above else (ih < nh - 1))
                there = jnp.logical_and(there, (iw > 0) if side == 0 else (iw < nw - 1))
                at_k = 4 * k + 2 * tt
                sf[side, t, pl.ds(0 if above else 18, 2), :] = jnp.where(there, v[at_k : at_k + 2], 0.0)

        sub = lax.broadcasted_iota(jnp.int32, (2, 8, CH), 1)

        for n in range(10 * lo, 10 * hi):
            t, h = n // 10, n % 10
            there = None if t >= 2 else it > 0
            if h in (0, 9):
                row = (ih > 0) if h == 0 else (ih < nh - 1)
                there = row if there is None else jnp.logical_and(there, row)
            x = cb[e, t, h].astype(F32).reshape(2, 8, CH)
            if norm is not None:
                x = silu((x - mean2) * scale2 + shift[None])
            if there is not None:
                x = jnp.where(there, x, 0.0)
            rims = [
                jnp.stack([sf[side, t, pl.ds(2 * h + c, 1), :] for c in (0, 1)])
                for side in (0, 1)
            ]
            before = jnp.where(sub == 0, rims[0], pltpu.roll(x, 1, 1))
            after = jnp.where(sub == 7, rims[1], pltpu.roll(x, 7, 1))
            for k, v in enumerate((before, x, after)):
                ab[t, h, :, pl.ds(k * CH, CH)] = v.reshape(16, CH).astype(BF16)

    def conv(kv, t0, t1):
        total = None
        for i in range(3):
            for j in range(3):
                part = jnp.dot(
                    ab[i + t0 : i + t1, j : j + 8].reshape(128 * (t1 - t0), 3 * CH), kv[3 * i + j], preferred_element_type=F32
                )
                total = part if total is None else total + part
        return total

    def keep(e, value, t0, t1):
        cb[e, 2 + t0 : 2 + t1, 1:9] = value.reshape(t1 - t0, 8, 16, CH).astype(BF16)
        fbuf[0, 128 * t0 : 128 * t1] = value[:, :128]
        fbuf[1, 128 * t0 : 128 * t1] = value[:, 128:]

    def fold():
        def step(n, _):
            t, rows = n // 16, pl.ds(pl.multiple_of((n % 16) * 16, 16), 16)
            cols = []
            for i in range(3):
                k = [kuv[t * 3 + i, j, rows, :].astype(F32) for j in range(3)]
                cols.append((k[0], k[1] + k[2], k[0] + k[1], k[2]))
            for c in range(4):
                v = [cols[i][c] for i in range(3)]
                for r, w in enumerate((v[0], v[1] + v[2], v[0] + v[1], v[2])):
                    kuc[(r // 2) * 2 + c // 2, t, r % 2, c % 2, rows, :] = w.astype(BF16)
            return 0

        lax.fori_loop(0, 48, step, 0)

    cells = 2 * 8 * 8
    total = cells * GROUP * nt * nh * nw
    loads[0].wait()
    x = jnp.stack([xv[c].astype(F32).reshape(2, 8, 8, CH) for c in (0, 1)], axis=2)
    row = moments(x, cells * GROUP)
    pl.semaphore_wait(barrier, len(plane) + len(line))
    gather(0, 0, g1, row, plane)
    keep(0, x.reshape(256, CH), 0, 2)
    onward, rows, cols = rims_out(0)
    corners(0)
    near = rows, cols, corners_out(0)
    row = merge(gathered(0, 0, g1, plane), cells * GROUP)
    gather(0, 1, g2, row, line)
    onward += rims_on(0, near)
    loads[2].wait()
    fold()
    row = merge(gathered(0, 1, g2, line), cells * GROUP * nh * nw)
    mean, rstd = spread_out(row, total)
    for c in onward:
        c.wait_recv()
    fill(0, (0, 4), (mean, [r * gain1[...] for r in rstd], shift1[...]))
    loads[1].wait()
    hidden = (conv(k1v, 0, 2) + bias1[...]).astype(BF16).astype(F32)

    row = moments(hidden.reshape(2, 8, 2, 8, CH), cells * GROUP)
    gather(1, 0, g3, row, pair)
    keep(1, hidden, 0, 2)
    onward, rows, cols = rims_out(1, False)
    row = merge(gathered(1, 0, g3, pair), cells * GROUP)
    g5[0] = row
    far = pltpu.make_async_remote_copy(
        src_ref=g5.at[0], dst_ref=g4.at[0], send_sem=gsend.at[1, 2], recv_sem=grecv.at[1, 2],
        device_id=at(nt // 2, 0, 0), device_id_type=MESH)

    @pl.when(core == 0)
    def _():
        g4[0] = row

    @pl.when(core == 1)
    def _():
        far.start()

    for slot, o in enumerate(chips):
        pltpu.make_async_remote_copy(
            src_ref=g5.at[0], dst_ref=g4.at[1 + slot], send_sem=gsend.at[1, 1], recv_sem=grecv.at[1, 1],
            device_id=(halfway[o[0]],) + at(*o)[1:], device_id_type=MESH).start()
    onward += frames_on(1, 0, 2, 8)
    corners(1)
    onward += rims_on(1, (rows, cols, corners_out(1)))

    @pl.when(core == 1)
    def _():
        far.wait_recv()
        far.wait_send()

    row = merge(gathered(1, 1, g4, chips), cells * GROUP * 2)
    gather(1, 3, g6, row, pair)
    row = merge(gathered(1, 3, g6, pair), cells * GROUP * nt * nh * nw // 2)
    mean, rstd = spread_out(row, total)
    for c in onward:
        c.wait_recv()
    fill(1, (0, 4), (mean, [r * gain2[...] for r in rstd], shift2[...]))
    loads[3].wait()
    earlier = list(sends)
    sends.clear()
    onward, near = [], []
    for t in (0, 1):
        skip = cb[0, 2 + t, 1:9].astype(F32).reshape(128, CH)
        residual = (conv(k2v, t, t + 1) + bias2[...] + skip).astype(BF16).astype(F32)
        keep(2, residual, t, t + 1)
        onward += frames_on(2, t, t + 1, 8 + 13 * t)
        near.append(rows_out(2, t, t + 1, 16 * t))
        columns(2, t, t + 1)
        near.append(columns_out(2, t, t + 1, 2 + 16 * t))
    corners(2)
    near.append(corners_out(2))
    first = onward[:1] + rows_on(2, 0, 1, 9, near[0]) + columns_on(2, 0, 1, 13, near[1])
    first += corners_on(2, near[4])
    second = onward[1:] + rows_on(2, 1, 2, 22, near[2]) + columns_on(2, 1, 2, 24, near[3])
    fill(2, (2, 4), None)
    up = bias_up[...]

    def window(t0, t1, a, b, r):
        return ab[t0:t1, a + r : a + r + 8, :, b * CH : (b + 2) * CH].reshape(128 * (t1 - t0), 2 * CH)

    def weight(a, b, i, r):
        return kuc[2 * a + b, i, r].reshape(2 * CH, CH)

    for a in (0, 1):
        for b in (0, 1):
            both = sum(jnp.dot(window(2, 4, a, b, r), weight(a, b, 2, r), preferred_element_type=F32) for r in (0, 1))
            late = sum(jnp.dot(window(2, 3, a, b, r), weight(a, b, 1, r), preferred_element_type=F32) for r in (0, 1))
            acc[2 * a + b, 0:128] = both[0:128] + up
            acc[2 * a + b, 128:256] = both[128:256] + late + up
    for c in earlier:
        c.wait_send()
    for c in first:
        c.wait_recv()
    fill(2, (0, 1), None)
    for a in (0, 1):
        for b in (0, 1):
            acc[2 * a + b, 0:128] += sum(
                jnp.dot(window(0, 1, a, b, r), weight(a, b, 0, r), preferred_element_type=F32) for r in (0, 1)
            )
    for c in second:
        c.wait_recv()
    fill(2, (1, 2), None)
    for a in (0, 1):
        for b in (0, 1):
            late, early = (
                sum(jnp.dot(window(1, 2, a, b, r), weight(a, b, i, r), preferred_element_type=F32) for r in (0, 1))
                for i in (0, 1)
            )
            done = [early + acc[2 * a + b, 0:128], late + acc[2 * a + b, 128:256]]
            for t in (0, 1):
                for half in (0, 1):
                    ob[a, half, pl.ds(256 * t + b, 128, stride=2), :] = done[t][:, half * 128 : half * 128 + 128]
        for n in range(32):
            t, h, c = n // 16, (n // 2) % 8, n % 2
            for half in (0, 1):
                out[c, t, 2 * h + a, :, pl.ds(half * 128, 128)] = ob[a, half, pl.ds(16 * n, 16), :].astype(BF16)
    for c in sends:
        c.wait_send()


def shards(sizes, latents, gain1, shift1, k1, bias1, gain2, shift2, k2, bias2, ku, bias_up):
    nt, nh, nw = sizes
    row = lambda v: v.reshape(1, CH)
    vmem = pl.BlockSpec(memory_space=pltpu.VMEM)
    hbm = pl.BlockSpec(memory_space=pl.ANY)
    s = pltpu.VMEM
    return pl.pallas_call(
        functools.partial(body, sizes),
        out_shape=pltpu.VMEM((2, 2, 16, 16, CH), BF16),
        in_specs=[hbm, vmem, vmem, hbm, vmem, vmem, vmem, hbm, vmem, hbm, vmem],
        out_specs=vmem,
        scratch_shapes=[
            s((2, 2, 64, CH), BF16),
            s((3, 4, 10, 16, CH), BF16),
            s((3, 2, 2, 32, CH), BF16),
            s((3, 16, CH), BF16),
            s((3, 4, 16, CH), BF16),
            s((3, 2, 16, CH), BF16),
            s((3, 2, 32, CH), BF16),
            s((2, 4, 20, CH), F32),
            s((4, 10, 16, 3 * CH), BF16),
            s((9, 3 * CH, CH), BF16),
            s((9, 3 * CH, CH), BF16),
            s((9, 3, CH, CH), BF16),
            s((4, 3, 2, 2, CH, CH), BF16),
            s((2, 264, 128), F32),
            s((4, 256, CH), F32),
            s((2, 2, 520, 128), F32),
            s((nh * nw, 1, 128), F32),
            s((nt, 1, 128), F32),
            s((2, 1, 128), F32),
            s((nt * nh * nw // 4, 1, 128), F32),
            s((1, 1, 128), F32),
            s((2, 1, 128), F32),
            pltpu.SemaphoreType.DMA((4,)),
            pltpu.SemaphoreType.DMA((3, 26)),
            pltpu.SemaphoreType.DMA((3, 26)),
            pltpu.SemaphoreType.DMA((2, 4)),
            pltpu.SemaphoreType.DMA((2, 4)),
        ],
        compiler_params=pltpu.CompilerParams(
            collective_id=0, has_side_effects=True, vmem_limit_bytes=62 * 2**20
        ),
        name="upblock",
    )(
        latents.reshape(2, 2, 64, CH), row(gain1), row(shift1), k1.reshape(9, 3 * CH, CH), row(bias1),
        row(gain2), row(shift2), k2.reshape(9, 3 * CH, CH), row(bias2), ku.reshape(9, 3, CH, CH), row(bias_up),
    )


def solution(mesh):
    sizes = tuple(mesh.shape[a] for a in AXES)
    in_specs = (P(None, "tm", "ha", "wa", None),) + (P(),) * 10
    return jax.shard_map(
        functools.partial(shards, sizes),
        mesh=mesh,
        in_specs=in_specs,
        out_specs=P(None, "tm", "ha", "wa", None),
        check_vma=False,
    )
```
